256 devices in a mesh: layer: 16 (over z_lo, y, core), ex: 16 (over z_hi, x).
Axes of the slice: x: 4, y: 4, z: 8 (z_hi: 4, z_lo: 2; z = z_hi * 2 + z_lo), core: 2. Of those that a mesh axis runs over, the one named last changes fastest.
Arguments:
- query_grads: bfloat16 [32, 512, 4096], P('layer', 'ex'), may hold values from -0.09375 to 0.09375
- train_grads: bfloat16 [32, 8192, 4096], P('layer', 'ex'), may hold values from -6 to 6
- basis_out: float32 [32, 64, 64], P('layer'), may hold values from -0.75 to 0.75
- basis_in: float32 [32, 64, 64], P('layer'), may hold values from -0.75 to 0.75
- eigen: float32 [32, 64, 64], P('layer'), may hold values from 0.0005 to 100, as said below
Outputs:
- scores: float32 [512, 8192], P('layer', 'ex')
The draws below stay inside these ranges and needn't reach their ends.
Inputs may be any that keep to these rules, and one draw needn't show every extreme that they name: eigen is positive.
All inputs are finite; a program needn't handle non-finite values.
Results may differ from the reference program's by a relative error of at most 0.0029.
Values may be sent and summed in bfloat16 or wider, within the bound.
No kernel may reach another device: no remote copies, remote signals or barrier semaphores. Data moves between devices by JAX's collectives and lax.ppermute only.
A program may use at most 128 MiB of HBM per device.

```python
import jax
import jax.numpy as jnp
from jax import lax

R = 64
MODULES = 32
TRAIN = 8192
QUERIES = 512


def draw_eigen(key, part):
    key = jax.random.fold_in(key, 11)
    key_rows, key_cols, key_elem = jax.random.split(key, 3)
    low, high, elem_low, elem_high = (0.1, 3.0, 0.5, 2.0)
    rows = jnp.exp(jax.random.uniform(key_rows, (MODULES, R, 1), jnp.float32, jnp.log(low), jnp.log(high)))
    cols = jnp.exp(jax.random.uniform(key_cols, (MODULES, 1, R), jnp.float32, jnp.log(low), jnp.log(high)))
    elem = jax.random.uniform(key_elem, (MODULES, R, R), jnp.float32, elem_low, elem_high)
    return (rows * cols * elem).astype(jnp.float32)


def block_levels(own_key, shape, cuts, low, largest):
    factor_of, own = 1.0, jax.random.fold_in(own_key, 6)
    for position, parts in cuts:
        steps = jnp.exp(jax.random.uniform(jax.random.fold_in(own, position), (parts,), jnp.float32, low / len(cuts), largest / len(cuts)))
        factor_of = factor_of * jnp.repeat(steps, shape[position] // parts).reshape([-1 if axis == position else 1 for axis in range(len(shape))])
    return factor_of


def normal_values(rng, shape, scale, reach, pieces=(), held_as=jnp.bfloat16):
    drawn = scale * jax.random.normal(rng, shape, jnp.float32)
    if pieces:
        drawn = drawn * block_levels(rng, shape, pieces, -0.22, 0.18)
    return jnp.clip(drawn, -reach, reach).astype(held_as)


def setup_inputs(seed: int = 0) -> dict:
    arg_keys = jax.random.split(jax.random.key(seed), 6)
    return {
        "query_grads": normal_values(arg_keys[0], (MODULES, QUERIES, R * R), 0.015625, 0.09375, ((0, 16), (1, 16))),
        "train_grads": normal_values(arg_keys[1], (MODULES, TRAIN, R * R), 1.0, 6.0, ((0, 16), (1, 16))),
        "basis_out": normal_values(arg_keys[2], (MODULES, R, R), R ** -0.5, 0.75, ((0, 16),), jnp.float32),
        "basis_in": normal_values(arg_keys[3], (MODULES, R, R), R ** -0.5, 0.75, ((0, 16),), jnp.float32),
        "eigen": draw_eigen(jax.random.fold_in(arg_keys[5], 71), 0),
    }


def precondition(raw, basis_out, basis_in, eigen):
    count_mod, count_q, entries = raw.shape
    side = basis_out.shape[1]
    hp = lax.Precision.HIGHEST
    grads = raw.reshape(count_mod, count_q, side, side).astype(jnp.float32)
    damping = 0.1 * jnp.mean(eigen, axis=(1, 2), keepdims=True)
    left = jnp.einsum('mai,mqab->mibq', basis_out, grads, precision=hp)
    rotated = jnp.einsum('mibq,mbj->mijq', left, basis_in, precision=hp)
    scaled = rotated / (eigen + damping)[:, :, :, None]
    back = jnp.einsum('mai,mijq->majq', basis_out, scaled, precision=hp)
    full = jnp.einsum('majq,mbj->mqab', back, basis_in, precision=hp)
    return full.reshape(count_mod, count_q, entries).astype(jnp.bfloat16)


def reference(query_grads, train_grads, basis_out, basis_in, eigen):
    precond = precondition(query_grads, basis_out, basis_in, eigen)

    def add_module(total, pair):
        ready, stored = pair
        term = lax.dot_general(ready.astype(jnp.float32), stored.astype(jnp.float32),
                               (((1,), (1,)), ((), ())), precision=lax.Precision.HIGHEST)
        return total + term, None

    start = jnp.zeros((precond.shape[1], train_grads.shape[1]), jnp.float32)
    total, unused = lax.scan(add_module, start, (precond, train_grads))
    return total
```

```python
import functools

import jax
import jax.numpy as jnp
from jax import lax
from jax.experimental import pallas as pl
from jax.experimental.pallas import tpu as pltpu
from jax.sharding import PartitionSpec as P

SIDE = 4


def precondition(raw, basis_out, basis_in, eigen):
    count_mod, count_q, entries = raw.shape
    side = basis_out.shape[1]
    prec = lax.Precision.HIGH
    grads = raw.reshape(count_mod, count_q, side, side).astype(jnp.float32)
    damping = 0.1 * jnp.mean(eigen, axis=(1, 2), keepdims=True)
    left = jnp.einsum("mai,mqab->mibq", basis_out, grads, precision=prec)
    rotated = jnp.einsum("mibq,mbj->mijq", left, basis_in, precision=prec)
    scaled = rotated / (eigen + damping)[:, :, :, None]
    back = jnp.einsum("mai,mijq->majq", basis_out, scaled, precision=prec)
    full = jnp.einsum("majq,mbj->mqab", back, basis_in, precision=prec)
    return full.reshape(count_mod, count_q, entries).astype(jnp.bfloat16)


def move_x(value, step):
    pairs = [(z * SIDE + x, z * SIDE + (x + step) % SIDE) for z in range(SIDE) for x in range(SIDE)]
    return lax.ppermute(value, "ex", pairs)


def move_z(value, step):
    pairs = [(z * SIDE + x, (z + step) % SIDE * SIDE + x) for z in range(SIDE) for x in range(SIDE)]
    return lax.ppermute(value, "ex", pairs)


def score_kernel(counts, *refs):
    shard_counts, done_counts, steps = counts
    places = refs[0] if done_counts else None
    refs = refs[1:] if done_counts else refs
    halves = sum(shard_counts)
    shards, train, done = refs[:halves], refs[halves], refs[halves + 1 : halves + 1 + len(done_counts)]
    out, total = refs[-2], refs[-1]
    module, step = pl.program_id(0), pl.program_id(1)

    rows, at = [], 0
    for count in shard_counts:
        if count == 1:
            rows.append(shards[at][0])
        else:
            rows.append(jnp.where(module == 0, shards[at][0], shards[at + 1][0]))
        at += count
    rows = jnp.concatenate(rows, axis=0)
    term = lax.dot_general(rows, train[0], (((1,), (1,)), ((), ())), preferred_element_type=jnp.float32)

    @pl.when((module == 0) & (step == 0))
    def _():
        total[...] = term

    @pl.when((module != 0) | (step != 0))
    def _():
        total[...] += term

    @pl.when((module == pl.num_programs(0) - 1) & (step == steps - 1))
    def _():
        blocks = total[...].astype(out.dtype).reshape((len(shard_counts),) + out.shape[1:])
        if not done_counts:
            out[...] = blocks
            return
        place = 0
        for ref, count in zip(done, done_counts):
            for i in range(count):
                out[places[place]] = ref[i]
                place += 1
        for i in range(len(shard_counts)):
            out[places[place]] = blocks[i]
            place += 1


def score_blocks(shards, train, done=(), places=None, tile=1024):
    modules, count_t, entries = train.shape
    shards = [s if isinstance(s, tuple) else (s,) for s in shards]
    count_q = shards[0][0].shape[1]
    shard_counts = tuple(len(s) for s in shards)
    done_counts = tuple(d.shape[0] for d in done)
    blocks = len(shards) + sum(done_counts)
    steps = entries // tile
    specs = []
    for s in shards:
        if len(s) == 1:
            specs.append(pl.BlockSpec((1, count_q, tile), lambda m, k, *_: (m, 0, k)))
        else:
            specs += [pl.BlockSpec((1, count_q, tile), lambda m, k, *_: (0, 0, k))] * 2
    specs.append(pl.BlockSpec((1, count_t, tile), lambda m, k, *_: (m, 0, k)))
    specs += [pl.BlockSpec(d.shape, lambda m, k, *_: (0, 0, 0)) for d in done]
    flat = [half for s in shards for half in s]
    prefetch = [places] if done else []
    rows = len(shards) * count_q
    return pl.pallas_call(
        functools.partial(score_kernel, (shard_counts, done_counts, steps)),
        out_shape=jax.ShapeDtypeStruct((blocks, count_q, count_t), jnp.bfloat16),
        grid_spec=pltpu.PrefetchScalarGridSpec(
            num_scalar_prefetch=len(prefetch),
            grid=(modules, steps),
            in_specs=specs,
            out_specs=pl.BlockSpec((blocks, count_q, count_t), lambda m, k, *_: (0, 0, 0)),
            scratch_shapes=[pltpu.VMEM((rows, count_t), jnp.float32)],
        ),
        compiler_params=pltpu.CompilerParams(vmem_limit_bytes=24 << 20),
        cost_estimate=pl.CostEstimate(
            flops=2 * rows * count_t * modules * entries,
            bytes_accessed=2 * modules * entries * (rows + count_t),
            transcendentals=0,
        ),
    )(*prefetch, *flat, train, *done)


def local(query_grads, train_grads, basis_out, basis_in, eigen):
    own = precondition(query_grads, basis_out, basis_in, eigen)
    zl, zr = move_z(own, 1), move_z(own, -1)
    xl, xr = move_x(own, 1), move_x(own, -1)
    x2 = (move_x(xl[:1], 1), move_x(xr[1:], -1))
    z2 = (move_z(zl[:1], 1), move_z(zr[1:], -1))
    zl_xl, zl_xr = move_x(zl, 1), move_x(zl, -1)
    zr_xl, zr_xr = move_x(zr, 1), move_x(zr, -1)
    x2 = jnp.concatenate(x2, axis=0)
    zl_x2, zr_x2 = move_z(x2, 1), move_z(x2, -1)
    z2 = jnp.concatenate(z2, axis=0)
    z2_xl, z2_xr = move_x(z2, 1), move_x(z2, -1)
    z2_x2 = (move_x(z2_xl[:1], 1), move_x(z2_xr[1:], -1))

    me = lax.axis_index("ex")
    z, x = lax.shift_right_logical(me, 2), me & 3
    steps = [
        (0, 0), (0, -1), (0, 1), (0, 2), (-1, 0), (1, 0),
        (-1, -1), (-1, 1), (1, -1), (1, 1), (2, 0), (-1, 2), (1, 2),
        (2, -1), (2, 1), (2, 2),
    ]
    away = jnp.array(steps, jnp.int32)
    places = ((z + away[:, 0]) & 3) * SIDE + ((x + away[:, 1]) & 3)
    first = score_blocks([own, xl, xr, x2, zl, zr], train_grads)
    second = score_blocks([zl_xl, zl_xr, zr_xl, zr_xr, z2, zl_x2, zr_x2], train_grads)
    parts = score_blocks([z2_xl, z2_xr, z2_x2], train_grads, (first, second), places)
    parts = lax.all_to_all(parts, "layer", split_axis=0, concat_axis=0, tiled=True)
    return jnp.sum(parts.astype(jnp.float32), axis=0)


def solution(mesh):
    in_specs = (
        P("layer", "ex", None),
        P("layer", "ex", None),
        P("layer", None, None),
        P("layer", None, None),
        P("layer", None, None),
    )
    out_specs = P("layer", "ex")
    return jax.shard_map(local, mesh=mesh, in_specs=in_specs, out_specs=out_specs, check_vma=False)
```

```python
import functools

import jax
import jax.numpy as jnp
from jax import lax
from jax.experimental import pallas as pl
from jax.experimental.pallas import tpu as pltpu
from jax.sharding import PartitionSpec as P

SIDE = 4
TILE = 2048

def split(v):
    hi = v.astype(jnp.bfloat16)
    return hi, (v - hi.astype(jnp.float32)).astype(jnp.bfloat16)

def twice(block):
    none = jnp.zeros_like(block)
    return jnp.concatenate([jnp.concatenate([block, none], axis=1), jnp.concatenate([none, block], axis=1)], axis=0)

def dot(a, b, dims=((1,), (0,))):
    return lax.dot_general(a, b, (dims, ((), ())), preferred_element_type=jnp.float32)

def precondition_kernel(raw, basis_out, basis_in, eigen, out, work):
    count_q, entries = raw.shape[1:]
    side = basis_out.shape[1]
    half = count_q // 2
    low = lax.broadcasted_iota(jnp.int32, (half, 2 * side), 1) < side

    out_hi, out_lo = split(basis_out[0])
    turned_hi, turned_lo = split(basis_out[0].T)
    in_hi, in_lo = split(twice(basis_in[0]))
    damped = eigen[0] + 0.1 * jnp.mean(eigen[0])
    inverse = 1.0 / damped
    inverse = jnp.concatenate([inverse, inverse], axis=1)

    rows = []
    for pair in range(side // 2):
        tile = raw[0, :, pl.ds(pair * 2 * side, 2 * side)].astype(jnp.float32)
        top, bottom = tile[:half], tile[half:]
        rows.append(jnp.where(low, top, pltpu.roll(bottom, side, 1)))
        rows.append(jnp.where(low, pltpu.roll(top, side, 1), bottom))
    grads = jnp.concatenate(rows, axis=0).astype(jnp.bfloat16)
    work[...] = dot(jnp.concatenate([grads, grads], axis=1), jnp.concatenate([in_hi, in_lo], axis=0))
    left = jnp.concatenate([work[pl.ds(q, side, stride=half), :] for q in range(half)], axis=1)
    hi, lo = split(left)
    rotated = dot(jnp.concatenate([turned_hi, turned_hi, turned_lo], axis=1), jnp.concatenate([hi, lo, hi], axis=0))
    scaled = jnp.concatenate([rotated[:, q * 2 * side : (q + 1) * 2 * side] * inverse for q in range(half)], axis=1)
    hi, lo = split(scaled)
    back = dot(jnp.concatenate([out_hi, out_hi, out_lo], axis=1), jnp.concatenate([hi, lo, hi], axis=0))
    back = jnp.concatenate([back[:, q * 2 * side : (q + 1) * 2 * side] for q in range(half)], axis=0)
    hi, lo = split(back)
    nt = ((1,), (1,))
    work[...] = dot(jnp.concatenate([hi, lo], axis=1), jnp.concatenate([in_hi, in_hi], axis=1), nt) + dot(hi, in_lo, nt)
    for pair in range(side // 2):
        even, odd = work[pl.ds(2 * pair, half, stride=side), :], work[pl.ds(2 * pair + 1, half, stride=side), :]
        at = pl.ds(pair * 2 * side, 2 * side)
        out[0, :half, at] = jnp.where(low, even, pltpu.roll(odd, side, 1)).astype(out.dtype)
        out[0, half:, at] = jnp.where(low, pltpu.roll(even, side, 1), odd).astype(out.dtype)

def precondition(raw, basis_out, basis_in, eigen):
    modules, count_q, entries = raw.shape
    side = basis_out.shape[1]
    per_module = lambda *shape: pl.BlockSpec((1,) + shape, lambda m: (m, 0, 0))
    return pl.pallas_call(
        precondition_kernel,
        out_shape=jax.ShapeDtypeStruct(raw.shape, jnp.bfloat16),
        grid=(modules,),
        in_specs=[per_module(count_q, entries)] + [per_module(side, side)] * 3,
        out_specs=per_module(count_q, entries),
        scratch_shapes=[pltpu.VMEM((side * count_q // 2, 2 * side), jnp.float32)],
        compiler_params=pltpu.CompilerParams(vmem_limit_bytes=56 << 20),
    )(raw, basis_out, basis_in, eigen)


def move(value, step_z, step_x):
    to = lambda z, x: (z + step_z) % SIDE * SIDE + (x + step_x) % SIDE
    return lax.ppermute(value, "ex", [(z * SIDE + x, to(z, x)) for z in range(SIDE) for x in range(SIDE)])


def in_order(*values):
    return lax.optimization_barrier(values)


def join_kernel(first, second, out):
    out[:1] = first[...]
    out[1:] = second[...]


def join(first, second):
    space = pl.BlockSpec(memory_space=pltpu.VMEM)
    return pl.pallas_call(
        join_kernel,
        out_shape=jax.ShapeDtypeStruct((2,) + first.shape[1:], first.dtype),
        in_specs=[space, space],
        out_specs=space,
        compiler_params=pltpu.CompilerParams(vmem_limit_bytes=4 << 20),
    )(first, second)


def scores_of(shards, train, modules):
    total = None
    for module in modules:
        for at in range(0, train.shape[2], TILE):
            part = pl.ds(at, TILE)
            rows = jnp.concatenate([s[0][module, :, part] if len(s) == 1 else s[module][0, :, part] for s in shards], axis=0)
            term = dot(train[module, :, part], rows, ((1,), (1,)))
            total = term if total is None else total + term
    return total


def blocks_of(total, shape, dtype):
    return total.T.astype(dtype).reshape((-1,) + shape)


def next_kernel(counts, *refs):
    shards, (train, out) = take(refs, counts)
    out[...] = blocks_of(scores_of(shards, train, range(train.shape[0])), out.shape[1:], out.dtype)


def last_kernel(counts, done_counts, offsets, me, *refs):
    shards, refs = take(refs, counts)
    train, done, out = refs[0], refs[1:-1], refs[-1]
    z, x = lax.shift_right_logical(me[0], 2), me[0] & (SIDE - 1)
    places = [((z + dz) & (SIDE - 1)) * SIDE + ((x + dx) & (SIDE - 1)) for dz, dx in offsets]
    at = 0
    for ref, count in zip(done, done_counts):
        for i in range(count):
            out[places[at]] = ref[i]
            at += 1
    blocks = blocks_of(scores_of(shards, train, range(train.shape[0])), out.shape[1:], out.dtype)
    for i in range(len(shards)):
        out[places[at + i]] = blocks[i]


def take(refs, counts):
    shards, at = [], 0
    for count in counts:
        shards.append(refs[at : at + count])
        at += count
    return shards, refs[at:]


def score_call(kernel, shards, others, other_specs, out_shapes, scratch=(), lead=()):
    shards = [s if isinstance(s, tuple) else (s,) for s in shards]
    flat = [half for s in shards for half in s]
    space = pl.BlockSpec(memory_space=pltpu.VMEM)
    train = next(o for o in others if o.ndim == 3 and o.dtype == flat[0].dtype)
    rows = len(shards) * flat[0].shape[1]
    return pl.pallas_call(
        functools.partial(kernel, tuple(len(s) for s in shards)),
        out_shape=out_shapes,
        in_specs=[pl.BlockSpec(memory_space=pltpu.SMEM)] * len(lead) + [space] * len(flat) + list(other_specs),
        out_specs=jax.tree.map(lambda _: space, out_shapes),
        scratch_shapes=list(scratch),
        compiler_params=pltpu.CompilerParams(vmem_limit_bytes=16 << 20),
        cost_estimate=pl.CostEstimate(
            flops=2 * rows * train.size,
            bytes_accessed=2 * (train.size + rows * train.size // train.shape[1]),
            transcendentals=0,
        ),
    )(*lead, *flat, *others)


def scores_next(shards, train):
    shape = (len(shards), shards[0].shape[1], train.shape[1])
    return score_call(
        next_kernel, shards, [train], [pl.BlockSpec(memory_space=pltpu.VMEM)], jax.ShapeDtypeStruct(shape, jnp.bfloat16)
    )


def scores_last(shards, train, done, offsets, me):
    counts = tuple(d.shape[0] for d in done)
    shape = (sum(counts) + len(shards),) + done[0].shape[1:]
    kernel = lambda own_counts, *refs: last_kernel(own_counts, counts, offsets, *refs)
    space = pl.BlockSpec(memory_space=pltpu.VMEM)
    return score_call(
        kernel,
        shards,
        [train, *done],
        [space] * (1 + len(done)),
        jax.ShapeDtypeStruct(shape, jnp.bfloat16),
        lead=[me],
    )


def local(query_grads, train_grads, basis_out, basis_in, eigen):
    me = lax.axis_index("ex").astype(jnp.int32).reshape(1)
    own = precondition(query_grads, basis_out, basis_in, eigen)
    zl, zr = move(own, 1, 0), move(own, -1, 0)
    xl, xr = move(own, 0, 1), move(own, 0, -1)
    x2 = move(own, 0, 2)
    zl, zr, xl, xr, x2 = in_order(zl, zr, xl, xr, x2)
    z2 = (move(zl[:1], 1, 0), move(zr[1:], -1, 0))
    zl_xl, zr_xr = move(zl, 0, 1), move(zr, 0, -1)
    first = scores_next([own, xl, xr, x2, zl, zr], train_grads)
    z2a, z2b, zl, zr, x2, zl_xl, zr_xr, first = in_order(*z2, zl, zr, x2, zl_xl, zr_xr, first)
    z2 = join(z2a, z2b)
    zl_x2, zr_x2 = move(x2[:1], 1, 0), move(x2[:1], -1, 0)
    z2_xl, z2_xr = move(z2, 0, 1), move(z2, 0, -1)
    z2_xl, z2_xr, zl, zr, x2, zl_x2, zr_x2 = in_order(z2_xl, z2_xr, zl, zr, x2, zl_x2, zr_x2)
    zl_x2, zr_x2 = (zl_x2, move(x2[1:], 1, 0)), (zr_x2, move(x2[1:], -1, 0))
    zr_xl, zl_xr = move(zr, 0, 1), move(zl, 0, -1)
    second = scores_next([zl_xl, zr_xr, z2, z2_xl, z2_xr], train_grads)
    z2_xl, z2_xr, second, zr_xl, zl_xr, *late = in_order(z2_xl, z2_xr, second, zr_xl, zl_xr, zl_x2[1], zr_x2[1])
    zl_x2, zr_x2 = (zl_x2[0], late[0]), (zr_x2[0], late[1])
    z2_x2 = (move(z2_xl[:1], 0, 1), move(z2_xr[1:], 0, -1))
    offsets = [
        (0, 0), (0, -1), (0, 1), (0, 2), (-1, 0), (1, 0),
        (-1, -1), (1, 1), (2, 0), (2, -1), (2, 1),
        (-1, 2), (1, 2), (2, 2), (1, -1), (-1, 1),
    ]
    parts = scores_last([zl_x2, zr_x2, z2_x2, zr_xl, zl_xr], train_grads, (first, second), offsets, me)
    parts = lax.all_to_all(parts, "layer", split_axis=0, concat_axis=0, tiled=True)
    return jnp.sum(parts.astype(jnp.float32), axis=0)


def solution(mesh):
    in_specs = (
        P("layer", "ex", None),
        P("layer", "ex", None),
        P("layer", None, None),
        P("layer", None, None),
        P("layer", None, None),
    )
    out_specs = P("layer", "ex")
    return jax.shard_map(local, mesh=mesh, in_specs=in_specs, out_specs=out_specs, check_vma=False)
```

```python
import functools

import jax
import jax.numpy as jnp
from jax import lax
from jax.experimental import pallas as pl
from jax.experimental.pallas import tpu as pltpu
from jax.sharding import PartitionSpec as P

SIDE = 4
TILE = 2048

def split(v):
    hi = v.astype(jnp.bfloat16)
    return hi, (v - hi.astype(jnp.float32)).astype(jnp.bfloat16)

def twice(block):
    none = jnp.zeros_like(block)
    return jnp.concatenate([jnp.concatenate([block, none], axis=1), jnp.concatenate([none, block], axis=1)], axis=0)

def dot(a, b, dims=((1,), (0,))):
    return lax.dot_general(a, b, (dims, ((), ())), preferred_element_type=jnp.float32)

def precondition_kernel(raw, basis_out, basis_in, eigen, out, work):
    count_q, entries = raw.shape[1:]
    side = basis_out.shape[1]
    half = count_q // 2
    low = lax.broadcasted_iota(jnp.int32, (half, 2 * side), 1) < side

    out_hi, out_lo = split(basis_out[0])
    turned_hi, turned_lo = split(basis_out[0].T)
    in_hi, in_lo = split(twice(basis_in[0]))
    damped = eigen[0] + 0.1 * jnp.mean(eigen[0])
    inverse = 1.0 / damped
    inverse = jnp.concatenate([inverse, inverse], axis=1)

    rows = []
    for pair in range(side // 2):
        tile = raw[0, :, pl.ds(pair * 2 * side, 2 * side)].astype(jnp.float32)
        top, bottom = tile[:half], tile[half:]
        rows.append(jnp.where(low, top, pltpu.roll(bottom, side, 1)))
        rows.append(jnp.where(low, pltpu.roll(top, side, 1), bottom))
    grads = jnp.concatenate(rows, axis=0).astype(jnp.bfloat16)
    work[...] = dot(jnp.concatenate([grads, grads], axis=1), jnp.concatenate([in_hi, in_lo], axis=0))
    left = jnp.concatenate([work[pl.ds(q, side, stride=half), :] for q in range(half)], axis=1)
    hi, lo = split(left)
    rotated = dot(jnp.concatenate([turned_hi, turned_hi, turned_lo], axis=1), jnp.concatenate([hi, lo, hi], axis=0))
    scaled = jnp.concatenate([rotated[:, q * 2 * side : (q + 1) * 2 * side] * inverse for q in range(half)], axis=1)
    hi, lo = split(scaled)
    back = dot(jnp.concatenate([out_hi, out_hi, out_lo], axis=1), jnp.concatenate([hi, lo, hi], axis=0))
    back = jnp.concatenate([back[:, q * 2 * side : (q + 1) * 2 * side] for q in range(half)], axis=0)
    hi, lo = split(back)
    nt = ((1,), (1,))
    work[...] = dot(jnp.concatenate([hi, lo], axis=1), jnp.concatenate([in_hi, in_hi], axis=1), nt) + dot(hi, in_lo, nt)
    for pair in range(side // 2):
        even, odd = work[pl.ds(2 * pair, half, stride=side), :], work[pl.ds(2 * pair + 1, half, stride=side), :]
        at = pl.ds(pair * 2 * side, 2 * side)
        out[0, :half, at] = jnp.where(low, even, pltpu.roll(odd, side, 1)).astype(out.dtype)
        out[0, half:, at] = jnp.where(low, pltpu.roll(even, side, 1), odd).astype(out.dtype)

def precondition(raw, basis_out, basis_in, eigen):
    modules, count_q, entries = raw.shape
    side = basis_out.shape[1]
    per_module = lambda *shape: pl.BlockSpec((1,) + shape, lambda m: (m, 0, 0))
    return pl.pallas_call(
        precondition_kernel,
        out_shape=jax.ShapeDtypeStruct(raw.shape, jnp.bfloat16),
        grid=(modules,),
        in_specs=[per_module(count_q, entries)] + [per_module(side, side)] * 3,
        out_specs=per_module(count_q, entries),
        scratch_shapes=[pltpu.VMEM((side * count_q // 2, 2 * side), jnp.float32)],
        compiler_params=pltpu.CompilerParams(vmem_limit_bytes=56 << 20),
    )(raw, basis_out, basis_in, eigen)


def move(value, step_z, step_x):
    to = lambda z, x: (z + step_z) % SIDE * SIDE + (x + step_x) % SIDE
    return lax.ppermute(value, "ex", [(z * SIDE + x, to(z, x)) for z in range(SIDE) for x in range(SIDE)])


def in_order(*values):
    return lax.optimization_barrier(values)


def join_kernel(first, second, out):
    out[:1] = first[...]
    out[1:] = second[...]


def join(first, second):
    space = pl.BlockSpec(memory_space=pltpu.VMEM)
    return pl.pallas_call(
        join_kernel,
        out_shape=jax.ShapeDtypeStruct((2,) + first.shape[1:], first.dtype),
        in_specs=[space, space],
        out_specs=space,
        compiler_params=pltpu.CompilerParams(vmem_limit_bytes=4 << 20),
    )(first, second)


def scores_of(shards, train, kept=None):
    total = None
    for module in range(train.shape[0]):
        for at in range(0, train.shape[2], TILE):
            part = pl.ds(at, TILE)
            held = train[module, :, part]
            if kept is not None:
                kept[module, :, part] = held
            rows = jnp.concatenate([s[0][module, :, part] if len(s) == 1 else s[module][0, :, part] for s in shards], axis=0)
            term = dot(held, rows, ((1,), (1,)))
            total = term if total is None else total + term
    return total


def blocks_of(total, shape, dtype):
    return total.T.astype(dtype).reshape((-1,) + shape)


def keep_kernel(counts, *refs):
    shards, (train, out, kept) = take(refs, counts)
    out[...] = blocks_of(scores_of(shards, train, kept), out.shape[1:], out.dtype)


def next_kernel(counts, *refs):
    shards, (train, out) = take(refs, counts)
    out[...] = blocks_of(scores_of(shards, train), out.shape[1:], out.dtype)


def last_kernel(counts, done_counts, offsets, me, *refs):
    shards, refs = take(refs, counts)
    train, done, out = refs[0], refs[1:-1], refs[-1]
    z, x = lax.shift_right_logical(me[0], 2), me[0] & (SIDE - 1)
    places = [((z + dz) & (SIDE - 1)) * SIDE + ((x + dx) & (SIDE - 1)) for dz, dx in offsets]
    at = 0
    for ref, count in zip(done, done_counts):
        for i in range(count):
            out[places[at]] = ref[i]
            at += 1
    blocks = blocks_of(scores_of(shards, train), out.shape[1:], out.dtype)
    for i in range(len(shards)):
        out[places[at + i]] = blocks[i]


def take(refs, counts):
    shards, at = [], 0
    for count in counts:
        shards.append(refs[at : at + count])
        at += count
    return shards, refs[at:]


def score_call(kernel, shards, train, out_shapes, others=(), lead=()):
    shards = [s if isinstance(s, tuple) else (s,) for s in shards]
    flat = [half for s in shards for half in s]
    space = pl.BlockSpec(memory_space=pltpu.VMEM)
    rows = len(shards) * flat[0].shape[1]
    return pl.pallas_call(
        functools.partial(kernel, tuple(len(s) for s in shards)),
        out_shape=out_shapes,
        in_specs=[pl.BlockSpec(memory_space=pltpu.SMEM)] * len(lead) + [space] * (len(flat) + 1 + len(others)),
        out_specs=jax.tree.map(lambda _: space, out_shapes),
        compiler_params=pltpu.CompilerParams(vmem_limit_bytes=16 << 20),
        cost_estimate=pl.CostEstimate(
            flops=2 * rows * train.size,
            bytes_accessed=2 * (train.size + rows * train.size // train.shape[1]),
            transcendentals=0,
        ),
    )(*lead, *flat, train, *others)


def blocks_shape(shards, train):
    return jax.ShapeDtypeStruct((len(shards), shards[0].shape[1], train.shape[1]), jnp.bfloat16)


def scores_keep(shards, train):
    kept = jax.ShapeDtypeStruct(train.shape, train.dtype)
    return score_call(keep_kernel, shards, train, [blocks_shape(shards, train), kept])


def scores_next(shards, train):
    return score_call(next_kernel, shards, train, blocks_shape(shards, train))


def scores_last(shards, train, done, offsets, me):
    counts = tuple(d.shape[0] for d in done)
    shape = (sum(counts) + len(shards),) + done[0].shape[1:]
    kernel = lambda own_counts, *refs: last_kernel(own_counts, counts, offsets, *refs)
    return score_call(kernel, shards, train, jax.ShapeDtypeStruct(shape, jnp.bfloat16), done, [me])


def local(query_grads, train_grads, basis_out, basis_in, eigen):
    me = lax.axis_index("ex").astype(jnp.int32).reshape(1)
    own = precondition(query_grads, basis_out, basis_in, eigen)
    x2 = move(own, 0, 2)
    xr, xl = move(own, 0, -1), move(own, 0, 1)
    zr, zl = move(own, -1, 0), move(own, 1, 0)
    zl, zr, xl, xr, x2 = in_order(zl, zr, xl, xr, x2)
    zr_xr, zl_xl = move(zr, 0, -1), move(zl, 0, 1)
    z2 = (move(zl[:1], 1, 0), move(zr[1:], -1, 0))
    first = scores_next([own, xl, xr, x2, zl, zr], train_grads)
    z2a, z2b, zl, zr, x2, zl_xl, zr_xr, first = in_order(*z2, zl, zr, x2, zl_xl, zr_xr, first)
    z2 = join(z2a, z2b)
    zr_xl = move(zr, 0, 1)
    z2_xl, z2_xr = move(z2, 0, 1), move(z2, 0, -1)
    zr_x2, zl_x2 = move(x2, -1, 0), move(x2, 1, 0)
    second = scores_next([zl_xl, zr_xr, z2], train_grads)
    z2_xr, zl = in_order(z2_xr, zl)
    zl_xr = move(zl, 0, -1)
    z2_xl, z2_xr, zr_xl, zl_xr, zl_x2, zr_x2, second = in_order(z2_xl, z2_xr, zr_xl, zl_xr, zl_x2, zr_x2, second)
    z2_x2 = (move(z2_xl[:1], 0, 1), move(z2_xr[1:], 0, -1))
    third, train = scores_keep([z2_xl, z2_xr, zr_xl, zl_xr, zl_x2, zr_x2], train_grads)
    third, train, *z2_x2 = in_order(third, train, *z2_x2)
    offsets = [
        (0, 0), (0, -1), (0, 1), (0, 2), (-1, 0), (1, 0),
        (-1, -1), (1, 1), (2, 0),
        (2, -1), (2, 1), (1, -1), (-1, 1), (-1, 2), (1, 2), (2, 2),
    ]
    parts = scores_last([tuple(z2_x2)], train, (first, second, third), offsets, me)
    parts = lax.all_to_all(parts, "layer", split_axis=0, concat_axis=0, tiled=True)
    return jnp.sum(parts.astype(jnp.float32), axis=0)


def solution(mesh):
    in_specs = (
        P("layer", "ex", None),
        P("layer", "ex", None),
        P("layer", None, None),
        P("layer", None, None),
        P("layer", None, None),
    )
    out_specs = P("layer", "ex")
    return jax.shard_map(local, mesh=mesh, in_specs=in_specs, out_specs=out_specs, check_vma=False)
```

```python
import functools

import jax
import jax.numpy as jnp
from jax import lax
from jax.experimental import pallas as pl
from jax.experimental.pallas import tpu as pltpu
from jax.sharding import PartitionSpec as P

SIDE = 4
TILE = 2048

def split(v):
    hi = v.astype(jnp.bfloat16)
    return hi, (v - hi.astype(jnp.float32)).astype(jnp.bfloat16)

def twice(block):
    none = jnp.zeros_like(block)
    return jnp.concatenate([jnp.concatenate([block, none], axis=1), jnp.concatenate([none, block], axis=1)], axis=0)

def dot(a, b, dims=((1,), (0,))):
    return lax.dot_general(a, b, (dims, ((), ())), preferred_element_type=jnp.float32)

def precondition_kernel(raw, basis_out, basis_in, eigen, out, work):
    count_q, entries = raw.shape[1:]
    side = basis_out.shape[1]
    half = count_q // 2
    low = lax.broadcasted_iota(jnp.int32, (half, 2 * side), 1) < side

    out_hi, out_lo = split(basis_out[0])
    turned_hi, turned_lo = split(basis_out[0].T)
    in_hi, in_lo = split(twice(basis_in[0]))
    damped = eigen[0] + 0.1 * jnp.mean(eigen[0])
    inverse = 1.0 / damped
    inverse = jnp.concatenate([inverse, inverse], axis=1)

    rows = []
    for pair in range(side // 2):
        tile = raw[0, :, pl.ds(pair * 2 * side, 2 * side)].astype(jnp.float32)
        top, bottom = tile[:half], tile[half:]
        rows.append(jnp.where(low, top, pltpu.roll(bottom, side, 1)))
        rows.append(jnp.where(low, pltpu.roll(top, side, 1), bottom))
    grads = jnp.concatenate(rows, axis=0).astype(jnp.bfloat16)
    work[...] = dot(jnp.concatenate([grads, grads], axis=1), jnp.concatenate([in_hi, in_lo], axis=0))
    left = jnp.concatenate([work[pl.ds(q, side, stride=half), :] for q in range(half)], axis=1)
    hi, lo = split(left)
    rotated = dot(jnp.concatenate([turned_hi, turned_hi, turned_lo], axis=1), jnp.concatenate([hi, lo, hi], axis=0))
    scaled = jnp.concatenate([rotated[:, q * 2 * side : (q + 1) * 2 * side] * inverse for q in range(half)], axis=1)
    hi, lo = split(scaled)
    back = dot(jnp.concatenate([out_hi, out_hi, out_lo], axis=1), jnp.concatenate([hi, lo, hi], axis=0))
    back = jnp.concatenate([back[:, q * 2 * side : (q + 1) * 2 * side] for q in range(half)], axis=0)
    hi, lo = split(back)
    nt = ((1,), (1,))
    work[...] = dot(jnp.concatenate([hi, lo], axis=1), jnp.concatenate([in_hi, in_hi], axis=1), nt) + dot(hi, in_lo, nt)
    for pair in range(side // 2):
        even, odd = work[pl.ds(2 * pair, half, stride=side), :], work[pl.ds(2 * pair + 1, half, stride=side), :]
        at = pl.ds(pair * 2 * side, 2 * side)
        out[0, :half, at] = jnp.where(low, even, pltpu.roll(odd, side, 1)).astype(out.dtype)
        out[0, half:, at] = jnp.where(low, pltpu.roll(even, side, 1), odd).astype(out.dtype)

def precondition(raw, basis_out, basis_in, eigen):
    modules, count_q, entries = raw.shape
    side = basis_out.shape[1]
    per_module = lambda *shape: pl.BlockSpec((1,) + shape, lambda m: (m, 0, 0))
    return pl.pallas_call(
        precondition_kernel,
        out_shape=jax.ShapeDtypeStruct(raw.shape, jnp.bfloat16),
        grid=(modules,),
        in_specs=[per_module(count_q, entries)] + [per_module(side, side)] * 3,
        out_specs=per_module(count_q, entries),
        scratch_shapes=[pltpu.VMEM((side * count_q // 2, 2 * side), jnp.float32)],
        compiler_params=pltpu.CompilerParams(vmem_limit_bytes=56 << 20),
    )(raw, basis_out, basis_in, eigen)


def move(value, step_z, step_x):
    to = lambda z, x: (z + step_z) % SIDE * SIDE + (x + step_x) % SIDE
    return lax.ppermute(value, "ex", [(z * SIDE + x, to(z, x)) for z in range(SIDE) for x in range(SIDE)])


def in_order(*values):
    return lax.optimization_barrier(values)


def arrange(values, plan):
    def kernel(*refs):
        given, made = refs[: len(values)], refs[len(values) :]
        for out, parts in zip(made, plan):
            for at, (value, module) in enumerate(parts):
                out[at] = given[value][module]

    space = pl.BlockSpec(memory_space=pltpu.VMEM)
    return pl.pallas_call(
        kernel,
        out_shape=[jax.ShapeDtypeStruct((len(parts),) + values[0].shape[1:], values[0].dtype) for parts in plan],
        in_specs=[space] * len(values),
        out_specs=[space] * len(plan),
        compiler_params=pltpu.CompilerParams(vmem_limit_bytes=4 << 20),
        cost_estimate=pl.CostEstimate(
            flops=0, bytes_accessed=4 * values[0][0].size * sum(len(parts) for parts in plan), transcendentals=0
        ),
    )(*values)


def blocks_of(shards, held, train, dtype, kept=None):
    total = None
    for module in range(train.shape[0]):
        for at in range(0, train.shape[2], TILE):
            part = pl.ds(at, TILE)
            stored = train[module, :, part]
            if kept is not None:
                kept[module, :, part] = stored
            rows = jnp.concatenate([held[s[module][0]][s[module][1], :, part] for s in shards], axis=0)
            term = dot(stored, rows, ((1,), (1,)))
            total = term if total is None else total + term
    return total.T.astype(dtype).reshape(len(shards), -1, train.shape[1])


def places_of(me, offsets):
    z, x = lax.shift_right_logical(me[0], 2), me[0] & (SIDE - 1)
    return [((z + dz) & (SIDE - 1)) * SIDE + ((x + dx) & (SIDE - 1)) for dz, dx in offsets]


def next_kernel(shards, count, *refs):
    held, (train, out) = refs[:count], refs[count:]
    out[...] = blocks_of(shards, held, train, out.dtype)


def place_kernel(shards, count, offsets, me, *refs):
    held, train, done, (out, kept) = refs[:count], refs[count], refs[count + 1 : -2], refs[-2:]
    places = places_of(me, offsets)
    at = 0
    for ref in done:
        for i in range(ref.shape[0]):
            out[places[at]] = ref[i]
            at += 1
    blocks = blocks_of(shards, held, train, out.dtype, kept)
    for i in range(len(shards)):
        out[places[at + i]] = blocks[i]


def last_kernel(shards, count, offsets, me, *refs):
    held, (train, _, out) = refs[:count], refs[count:]
    blocks = blocks_of(shards, held, train, out.dtype)
    for i, place in enumerate(places_of(me, offsets)):
        out[place] = blocks[i]


def score_call(kernel, shards, train, out_shapes, others=(), lead=(), aliases=None):
    arrays = []
    for array in (array for shard in shards for array, _ in shard):
        if all(array is not a for a in arrays):
            arrays.append(array)
    number = lambda array: next(i for i, a in enumerate(arrays) if a is array)
    shards = [[(number(array), at) for array, at in shard] for shard in shards]
    space = pl.BlockSpec(memory_space=pltpu.VMEM)
    rows = len(shards) * arrays[0].shape[1]
    return pl.pallas_call(
        functools.partial(kernel, shards, len(arrays)),
        out_shape=out_shapes,
        in_specs=[pl.BlockSpec(memory_space=pltpu.SMEM)] * len(lead) + [space] * (len(arrays) + 1 + len(others)),
        out_specs=jax.tree.map(lambda _: space, out_shapes),
        input_output_aliases={len(lead) + len(arrays) + 1: 0} if aliases else {},
        compiler_params=pltpu.CompilerParams(vmem_limit_bytes=16 << 20),
        cost_estimate=pl.CostEstimate(
            flops=2 * rows * train.size,
            bytes_accessed=2 * (train.size + rows * train.size // train.shape[1]),
            transcendentals=0,
        ),
    )(*lead, *arrays, train, *others)


def shard(array, at=0):
    return [(array, at), (array, at + 1)]


def blocks_shape(count, train, queries):
    return jax.ShapeDtypeStruct((count, queries, train.shape[1]), jnp.bfloat16)


def local(query_grads, train_grads, basis_out, basis_in, eigen):
    me = lax.axis_index("ex").astype(jnp.int32).reshape(1)
    queries = query_grads.shape[1]
    own = precondition(query_grads, basis_out, basis_in, eigen)
    xr, xl = move(own, 0, -1), move(own, 0, 1)
    zr, zl = move(own, -1, 0), move(own, 1, 0)
    halves = arrange([xl, xr], [[(0, 0)], [(1, 1)]])
    x2 = move(halves[1], 0, -1), move(halves[0], 0, 1)
    zl, zr, x2b, x2a = in_order(zl, zr, *x2)
    plan = [[(0, 0)], [(1, 1)], [(0, 0), (0, 1), (1, 0), (1, 1)], [(2, 0), (3, 0)]]
    zl_half, zr_half, both, x2 = arrange([zl, zr, x2a, x2b], plan)
    both_xr, both_xl = move(both, 0, -1), move(both, 0, 1)
    z2b, z2a = move(zr_half, -1, 0), move(zl_half, 1, 0)
    shards = [shard(own), shard(xl), shard(xr), shard(x2), shard(both, 0), shard(both, 2)]
    first = score_call(next_kernel, shards, train_grads, blocks_shape(6, train_grads, queries))
    z2a, z2b, x2, first = in_order(z2a, z2b, x2, first)
    (z2,) = arrange([z2a, z2b], [[(0, 0), (1, 0)]])
    z2_xl = move(z2, 0, 1)
    zr_x2, zl_x2 = move(x2, -1, 0), move(x2, 1, 0)
    z2, both_xr = in_order(z2, both_xr)
    z2_xr = move(z2, 0, -1)
    shards = [shard(z2), shard(both_xr, 0), shard(both_xr, 2)]
    second = score_call(next_kernel, shards, train_grads, blocks_shape(3, train_grads, queries))
    z2_xl, z2_xr, both_xl, zl_x2, zr_x2, second = in_order(z2_xl, z2_xr, both_xl, zl_x2, zr_x2, second)
    halves = arrange([z2_xl, z2_xr], [[(0, 0)], [(1, 1)]])
    z2_x2 = move(halves[0], 0, 1), move(halves[1], 0, -1)
    offsets = [
        (0, 0), (0, -1), (0, 1), (0, 2), (-1, 0), (1, 0),
        (2, 0), (-1, 1), (1, 1),
        (2, -1), (2, 1), (-1, -1), (1, -1), (-1, 2), (1, 2),
        (2, 2),
    ]
    shards = [shard(z2_xl), shard(z2_xr), shard(both_xl, 0), shard(both_xl, 2), shard(zl_x2), shard(zr_x2)]
    shapes = [blocks_shape(SIDE * SIDE, train_grads, queries), jax.ShapeDtypeStruct(train_grads.shape, train_grads.dtype)]
    kernel = lambda own, count, *refs: place_kernel(own, count, offsets[:-1], *refs)
    parts, train = score_call(kernel, shards, train_grads, shapes, [first, second], [me])
    parts, train, *z2_x2 = in_order(parts, train, *z2_x2)
    kernel = lambda own, count, *refs: last_kernel(own, count, offsets[-1:], *refs)
    shards = [[(half, 0) for half in z2_x2]]
    parts = score_call(kernel, shards, train, shapes[0], [parts], [me], True)
    parts = lax.all_to_all(parts, "layer", split_axis=0, concat_axis=0, tiled=True)
    return jnp.sum(parts.astype(jnp.float32), axis=0)


def solution(mesh):
    in_specs = (
        P("layer", "ex", None),
        P("layer", "ex", None),
        P("layer", None, None),
        P("layer", None, None),
        P("layer", None, None),
    )
    out_specs = P("layer", "ex")
    return jax.shard_map(local, mesh=mesh, in_specs=in_specs, out_specs=out_specs, check_vma=False)
```

```python
import functools

import jax
import jax.numpy as jnp
from jax import lax
from jax.experimental import pallas as pl
from jax.experimental.pallas import tpu as pltpu
from jax.sharding import PartitionSpec as P

SIDE = 4
TILE = 2048

def split(v):
    hi = v.astype(jnp.bfloat16)
    return hi, (v - hi.astype(jnp.float32)).astype(jnp.bfloat16)

def twice(block):
    none = jnp.zeros_like(block)
    return jnp.concatenate([jnp.concatenate([block, none], axis=1), jnp.concatenate([none, block], axis=1)], axis=0)

def dot(a, b, dims=((1,), (0,))):
    return lax.dot_general(a, b, (dims, ((), ())), preferred_element_type=jnp.float32)

def precondition_kernel(raw, basis_out, basis_in, eigen, out, work):
    modules, count_q, entries = raw.shape
    side = basis_out.shape[1]
    half = count_q // 2
    low = lax.broadcasted_iota(jnp.int32, (half, 2 * side), 1) < side
    every = range(modules)
    nt = ((1,), (1,))

    outs = [split(basis_out[m]) for m in every]
    turned = [split(basis_out[m].T) for m in every]
    ins = [split(twice(basis_in[m])) for m in every]
    inverses = [1.0 / (eigen[m] + 0.1 * jnp.mean(eigen[m])) for m in every]
    inverses = [jnp.concatenate([v, v], axis=1) for v in inverses]
    for m in every:
        rows = []
        for pair in range(side // 2):
            tile = raw[m, :, pl.ds(pair * 2 * side, 2 * side)].astype(jnp.float32)
            top, bottom = tile[:half], tile[half:]
            rows.append(jnp.where(low, top, pltpu.roll(bottom, side, 1)))
            rows.append(jnp.where(low, pltpu.roll(top, side, 1), bottom))
        grads = jnp.concatenate(rows, axis=0).astype(jnp.bfloat16)
        work[m] = dot(jnp.concatenate([grads, grads], axis=1), jnp.concatenate(ins[m], axis=0))
    parts = []
    for m in every:
        left = jnp.concatenate([work[m, pl.ds(q, side, stride=half), :] for q in range(half)], axis=1)
        hi, lo = split(left)
        parts.append((hi, lo))
    rotated = []
    for m in every:
        (hi, lo), (t_hi, t_lo) = parts[m], turned[m]
        rotated.append(dot(jnp.concatenate([t_hi, t_hi, t_lo], axis=1), jnp.concatenate([hi, lo, hi], axis=0)))
    scaled = []
    for m in every:
        blocks = [rotated[m][:, q * 2 * side : (q + 1) * 2 * side] * inverses[m] for q in range(half)]
        scaled.append(split(jnp.concatenate(blocks, axis=1)))
    back = []
    for m in every:
        (hi, lo), (o_hi, o_lo) = scaled[m], outs[m]
        back.append(dot(jnp.concatenate([o_hi, o_hi, o_lo], axis=1), jnp.concatenate([hi, lo, hi], axis=0)))
    for m in every:
        hi, lo = split(jnp.concatenate([back[m][:, q * 2 * side : (q + 1) * 2 * side] for q in range(half)], axis=0))
        in_hi, in_lo = ins[m]
        work[m] = dot(jnp.concatenate([hi, lo], axis=1), jnp.concatenate([in_hi, in_hi], axis=1), nt) + dot(hi, in_lo, nt)
    for m in every:
        for pair in range(side // 2):
            even, odd = work[m, pl.ds(2 * pair, half, stride=side), :], work[m, pl.ds(2 * pair + 1, half, stride=side), :]
            at = pl.ds(pair * 2 * side, 2 * side)
            out[m, :half, at] = jnp.where(low, even, pltpu.roll(odd, side, 1)).astype(out.dtype)
            out[m, half:, at] = jnp.where(low, pltpu.roll(even, side, 1), odd).astype(out.dtype)

def precondition(raw, basis_out, basis_in, eigen):
    modules, count_q, entries = raw.shape
    side = basis_out.shape[1]
    full = lambda *shape: pl.BlockSpec(shape, lambda i: (0, 0, 0))
    return pl.pallas_call(
        precondition_kernel,
        out_shape=jax.ShapeDtypeStruct(raw.shape, jnp.bfloat16),
        grid=(1,),
        in_specs=[full(*raw.shape)] + [full(modules, side, side)] * 3,
        out_specs=full(*raw.shape),
        scratch_shapes=[pltpu.VMEM((modules, side * count_q // 2, 2 * side), jnp.float32)],
        compiler_params=pltpu.CompilerParams(vmem_limit_bytes=56 << 20),
    )(raw, basis_out, basis_in, eigen)


def move(value, step_z, step_x):
    to = lambda z, x: (z + step_z) % SIDE * SIDE + (x + step_x) % SIDE
    return lax.ppermute(value, "ex", [(z * SIDE + x, to(z, x)) for z in range(SIDE) for x in range(SIDE)])


def in_order(*values):
    return lax.optimization_barrier(values)


def arrange(values, plan):
    def kernel(*refs):
        given, made = refs[: len(values)], refs[len(values) :]
        for out, parts in zip(made, plan):
            for at, (value, module) in enumerate(parts):
                out[at] = given[value][module]

    space = pl.BlockSpec(memory_space=pltpu.VMEM)
    return pl.pallas_call(
        kernel,
        out_shape=[jax.ShapeDtypeStruct((len(parts),) + values[0].shape[1:], values[0].dtype) for parts in plan],
        in_specs=[space] * len(values),
        out_specs=[space] * len(plan),
        compiler_params=pltpu.CompilerParams(vmem_limit_bytes=4 << 20),
        cost_estimate=pl.CostEstimate(
            flops=0, bytes_accessed=4 * values[0][0].size * sum(len(parts) for parts in plan), transcendentals=0
        ),
    )(*values)


def blocks_of(shards, held, train, dtype, kept=None):
    total = None
    for module in range(train.shape[0]):
        for at in range(0, train.shape[2], TILE):
            part = pl.ds(at, TILE)
            stored = train[module, :, part]
            if kept is not None:
                kept[module, :, part] = stored
            rows = jnp.concatenate([held[s[module][0]][s[module][1], :, part] for s in shards], axis=0)
            term = dot(stored, rows, ((1,), (1,)))
            total = term if total is None else total + term
    return total.T.astype(dtype).reshape(len(shards), -1, train.shape[1])


def next_kernel(shards, count, *refs):
    held, (train, out) = refs[:count], refs[count:]
    out[...] = blocks_of(shards, held, train, out.dtype)


def keep_kernel(shards, count, *refs):
    held, (train, out, kept) = refs[:count], refs[count:]
    out[...] = blocks_of(shards, held, train, out.dtype, kept)


def last_kernel(shards, count, offsets, me, *refs):
    held, train, done, out = refs[:count], refs[count], refs[count + 1 : -1], refs[-1]
    z, x = lax.shift_right_logical(me[0], 2), me[0] & (SIDE - 1)
    places = [((z + dz) & (SIDE - 1)) * SIDE + ((x + dx) & (SIDE - 1)) for dz, dx in offsets]
    at = 0
    for ref in done:
        for i in range(ref.shape[0]):
            out[places[at]] = ref[i]
            at += 1
    blocks = blocks_of(shards, held, train, out.dtype)
    for i in range(len(shards)):
        out[places[at + i]] = blocks[i]


def score_call(kernel, shards, train, out_shapes, others=(), lead=(), weight=1):
    arrays = []
    for array in (array for shard in shards for array, _ in shard):
        if all(array is not a for a in arrays):
            arrays.append(array)
    number = lambda array: next(i for i, a in enumerate(arrays) if a is array)
    shards = [[(number(array), at) for array, at in shard] for shard in shards]
    space = pl.BlockSpec(memory_space=pltpu.VMEM)
    rows = len(shards) * arrays[0].shape[1]
    return pl.pallas_call(
        functools.partial(kernel, shards, len(arrays)),
        out_shape=out_shapes,
        in_specs=[pl.BlockSpec(memory_space=pltpu.SMEM)] * len(lead) + [space] * (len(arrays) + 1 + len(others)),
        out_specs=jax.tree.map(lambda _: space, out_shapes),
        compiler_params=pltpu.CompilerParams(vmem_limit_bytes=16 << 20),
        cost_estimate=pl.CostEstimate(
            flops=2 * rows * train.size * weight,
            bytes_accessed=2 * (train.size + rows * train.size // train.shape[1]),
            transcendentals=0,
        ),
    )(*lead, *arrays, train, *others)


def shard(array, at=0):
    return [(array, at), (array, at + 1)]


def blocks_shape(count, train, queries):
    return jax.ShapeDtypeStruct((count, queries, train.shape[1]), jnp.bfloat16)


def local(query_grads, train_grads, basis_out, basis_in, eigen):
    me = lax.axis_index("ex").astype(jnp.int32).reshape(1)
    queries = query_grads.shape[1]
    own = precondition(query_grads, basis_out, basis_in, eigen)
    x2 = move(own, 0, 2)
    xr, xl = move(own, 0, -1), move(own, 0, 1)
    zr, zl = move(own, -1, 0), move(own, 1, 0)
    zl, zr, xl, xr = in_order(zl, zr, xl, xr)
    zl_half, zr_half, both = arrange([zl, zr], [[(0, 0)], [(1, 1)], [(0, 0), (0, 1), (1, 0), (1, 1)]])
    both_xr, both_xl = move(both, 0, -1), move(both, 0, 1)
    z2b, z2a = move(zr_half, -1, 0), move(zl_half, 1, 0)
    shards = [shard(own), shard(xl), shard(xr), shard(x2), shard(both, 0), shard(both, 2)]
    first = score_call(next_kernel, shards, train_grads, blocks_shape(6, train_grads, queries), weight=4)
    z2a, z2b, x2, first = in_order(z2a, z2b, x2, first)
    (z2,) = arrange([z2a, z2b], [[(0, 0), (1, 0)]])
    z2_xl = move(z2, 0, 1)
    zr_x2, zl_x2 = move(x2, -1, 0), move(x2, 1, 0)
    z2, both_xr = in_order(z2, both_xr)
    z2_xr = move(z2, 0, -1)
    shards = [shard(z2), shard(both_xr, 0), shard(both_xr, 2)]
    second = score_call(next_kernel, shards, train_grads, blocks_shape(3, train_grads, queries))
    z2_xl, z2_xr, both_xl, zl_x2, zr_x2, second = in_order(z2_xl, z2_xr, both_xl, zl_x2, zr_x2, second)
    halves = arrange([z2_xl, z2_xr], [[(0, 0)], [(1, 1)]])
    z2_x2 = move(halves[0], 0, 1), move(halves[1], 0, -1)
    offsets = [
        (0, 0), (0, -1), (0, 1), (0, 2), (-1, 0), (1, 0),
        (2, 0), (-1, 1), (1, 1),
        (2, -1), (-1, -1), (1, -1),
        (2, 1), (-1, 2), (1, 2), (2, 2),
    ]
    shards = [shard(z2_xl), shard(both_xl, 0), shard(both_xl, 2)]
    shapes = [blocks_shape(3, train_grads, queries), jax.ShapeDtypeStruct(train_grads.shape, train_grads.dtype)]
    third, train = score_call(keep_kernel, shards, train_grads, shapes)
    third, train, *z2_x2 = in_order(third, train, *z2_x2)
    shards = [shard(z2_xr), shard(zl_x2), shard(zr_x2), [(half, 0) for half in z2_x2]]
    kernel = lambda own, count, *refs: last_kernel(own, count, offsets, *refs)
    shape = blocks_shape(SIDE * SIDE, train_grads, queries)
    parts = score_call(kernel, shards, train, shape, [first, second, third], [me])
    parts = lax.all_to_all(parts, "layer", split_axis=0, concat_axis=0, tiled=True)
    return jnp.sum(parts.astype(jnp.float32), axis=0)


def solution(mesh):
    in_specs = (
        P("layer", "ex", None),
        P("layer", "ex", None),
        P("layer", None, None),
        P("layer", None, None),
        P("layer", None, None),
    )
    out_specs = P("layer", "ex")
    return jax.shard_map(local, mesh=mesh, in_specs=in_specs, out_specs=out_specs, check_vma=False)
```

```python
import functools

import jax
import jax.numpy as jnp
from jax import lax
from jax.experimental import pallas as pl
from jax.experimental.pallas import tpu as pltpu
from jax.sharding import PartitionSpec as P

SIDE = 4
TILE = 2048

def split(v):
    hi = v.astype(jnp.bfloat16)
    return hi, (v - hi.astype(jnp.float32)).astype(jnp.bfloat16)

def twice(block):
    none = jnp.zeros_like(block)
    return jnp.concatenate([jnp.concatenate([block, none], axis=1), jnp.concatenate([none, block], axis=1)], axis=0)

def dot(a, b, dims=((1,), (0,))):
    return lax.dot_general(a, b, (dims, ((), ())), preferred_element_type=jnp.float32)

def precondition_kernel(raw, basis_out, basis_in, eigen, out, work):
    modules, count_q, entries = raw.shape
    side = basis_out.shape[1]
    half = count_q // 2
    low = lax.broadcasted_iota(jnp.int32, (half, 2 * side), 1) < side
    every = range(modules)
    nt = ((1,), (1,))

    outs = [split(basis_out[m]) for m in every]
    turned = [split(basis_out[m].T) for m in every]
    ins = [split(twice(basis_in[m])) for m in every]
    inverses = [1.0 / (eigen[m] + 0.1 * jnp.mean(eigen[m])) for m in every]
    inverses = [jnp.concatenate([v, v], axis=1) for v in inverses]
    for m in every:
        rows = []
        for pair in range(side // 2):
            tile = raw[m, :, pl.ds(pair * 2 * side, 2 * side)].astype(jnp.float32)
            top, bottom = tile[:half], tile[half:]
            rows.append(jnp.where(low, top, pltpu.roll(bottom, side, 1)))
            rows.append(jnp.where(low, pltpu.roll(top, side, 1), bottom))
        grads = jnp.concatenate(rows, axis=0).astype(jnp.bfloat16)
        work[m] = dot(jnp.concatenate([grads, grads], axis=1), jnp.concatenate(ins[m], axis=0))
    parts = []
    for m in every:
        left = jnp.concatenate([work[m, pl.ds(q, side, stride=half), :] for q in range(half)], axis=1)
        hi, lo = split(left)
        parts.append((hi, lo))
    rotated = []
    for m in every:
        (hi, lo), (t_hi, t_lo) = parts[m], turned[m]
        rotated.append(dot(jnp.concatenate([t_hi, t_hi, t_lo], axis=1), jnp.concatenate([hi, lo, hi], axis=0)))
    scaled = []
    for m in every:
        blocks = [rotated[m][:, q * 2 * side : (q + 1) * 2 * side] * inverses[m] for q in range(half)]
        scaled.append(split(jnp.concatenate(blocks, axis=1)))
    back = []
    for m in every:
        (hi, lo), (o_hi, o_lo) = scaled[m], outs[m]
        back.append(dot(jnp.concatenate([o_hi, o_hi, o_lo], axis=1), jnp.concatenate([hi, lo, hi], axis=0)))
    for m in every:
        hi, lo = split(jnp.concatenate([back[m][:, q * 2 * side : (q + 1) * 2 * side] for q in range(half)], axis=0))
        in_hi, in_lo = ins[m]
        work[m] = dot(jnp.concatenate([hi, lo], axis=1), jnp.concatenate([in_hi, in_hi], axis=1), nt) + dot(hi, in_lo, nt)
    for m in every:
        for pair in range(side // 2):
            even, odd = work[m, pl.ds(2 * pair, half, stride=side), :], work[m, pl.ds(2 * pair + 1, half, stride=side), :]
            at = pl.ds(pair * 2 * side, 2 * side)
            out[m, :half, at] = jnp.where(low, even, pltpu.roll(odd, side, 1)).astype(out.dtype)
            out[m, half:, at] = jnp.where(low, pltpu.roll(even, side, 1), odd).astype(out.dtype)

def precondition(raw, basis_out, basis_in, eigen):
    modules, count_q, entries = raw.shape
    side = basis_out.shape[1]
    full = lambda *shape: pl.BlockSpec(shape, lambda i: (0, 0, 0))
    return pl.pallas_call(
        precondition_kernel,
        out_shape=jax.ShapeDtypeStruct(raw.shape, jnp.bfloat16),
        grid=(1,),
        in_specs=[full(*raw.shape)] + [full(modules, side, side)] * 3,
        out_specs=full(*raw.shape),
        scratch_shapes=[pltpu.VMEM((modules, side * count_q // 2, 2 * side), jnp.float32)],
        compiler_params=pltpu.CompilerParams(vmem_limit_bytes=56 << 20),
    )(raw, basis_out, basis_in, eigen)


def move(value, step_z, step_x):
    to = lambda z, x: (z + step_z) % SIDE * SIDE + (x + step_x) % SIDE
    return lax.ppermute(value, "ex", [(z * SIDE + x, to(z, x)) for z in range(SIDE) for x in range(SIDE)])


def in_order(*values):
    return lax.optimization_barrier(values)


def cost(weight):
    return pl.CostEstimate(flops=int(weight * 1.1e9), bytes_accessed=1024, transcendentals=0)


def arrange(values, plan, weight=0):
    def kernel(*refs):
        given, made = refs[: len(values)], refs[len(values) :]
        for out, parts in zip(made, plan):
            for at, (value, module) in enumerate(parts):
                out[at] = given[value][module]

    space = pl.BlockSpec(memory_space=pltpu.VMEM)
    return pl.pallas_call(
        kernel,
        out_shape=[jax.ShapeDtypeStruct((len(parts),) + values[0].shape[1:], values[0].dtype) for parts in plan],
        in_specs=[space] * len(values),
        out_specs=[space] * len(plan),
        compiler_params=pltpu.CompilerParams(vmem_limit_bytes=4 << 20),
        cost_estimate=cost(weight),
    )(*values)


def blocks_of(shards, held, train, dtype, kept=None):
    total = None
    for module in range(train.shape[0]):
        for at in range(0, train.shape[2], TILE):
            part = pl.ds(at, TILE)
            stored = train[module, :, part]
            if kept is not None:
                kept[module, :, part] = stored
            rows = jnp.concatenate([held[s[module][0]][s[module][1], :, part] for s in shards], axis=0)
            term = dot(stored, rows, ((1,), (1,)))
            total = term if total is None else total + term
    return total.T.astype(dtype).reshape(len(shards), -1, train.shape[1])


def next_kernel(shards, count, *refs):
    held, (train, out) = refs[:count], refs[count:]
    out[...] = blocks_of(shards, held, train, out.dtype)


def keep_kernel(shards, count, *refs):
    held, (train, out, kept) = refs[:count], refs[count:]
    out[...] = blocks_of(shards, held, train, out.dtype, kept)


def last_kernel(shards, count, offsets, me, *refs):
    held, train, done, out = refs[:count], refs[count], refs[count + 1 : -1], refs[-1]
    z, x = lax.shift_right_logical(me[0], 2), me[0] & (SIDE - 1)
    places = [((z + dz) & (SIDE - 1)) * SIDE + ((x + dx) & (SIDE - 1)) for dz, dx in offsets]
    at = 0
    for ref in done:
        for i in range(ref.shape[0]):
            out[places[at]] = ref[i]
            at += 1
    blocks = blocks_of(shards, held, train, out.dtype)
    for i in range(len(shards)):
        out[places[at + i]] = blocks[i]


def score_call(kernel, shards, train, out_shapes, others=(), lead=(), weight=1):
    arrays = []
    for array in (array for shard in shards for array, _ in shard):
        if all(array is not a for a in arrays):
            arrays.append(array)
    number = lambda array: next(i for i, a in enumerate(arrays) if a is array)
    shards = [[(number(array), at) for array, at in shard] for shard in shards]
    space = pl.BlockSpec(memory_space=pltpu.VMEM)
    return pl.pallas_call(
        functools.partial(kernel, shards, len(arrays)),
        out_shape=out_shapes,
        in_specs=[pl.BlockSpec(memory_space=pltpu.SMEM)] * len(lead) + [space] * (len(arrays) + 1 + len(others)),
        out_specs=jax.tree.map(lambda _: space, out_shapes),
        compiler_params=pltpu.CompilerParams(vmem_limit_bytes=16 << 20),
        cost_estimate=cost(weight),
    )(*lead, *arrays, train, *others)


def shard(array, at=0):
    return [(array, at), (array, at + 1)]


def blocks_shape(count, train, queries):
    return jax.ShapeDtypeStruct((count, queries, train.shape[1]), jnp.bfloat16)


def local(query_grads, train_grads, basis_out, basis_in, eigen):
    me = lax.axis_index("ex").astype(jnp.int32).reshape(1)
    queries = query_grads.shape[1]
    own = precondition(query_grads, basis_out, basis_in, eigen)
    x2 = move(own, 0, 2)
    xr, xl = move(own, 0, -1), move(own, 0, 1)
    zr, zl = move(own, -1, 0), move(own, 1, 0)
    zl, zr = in_order(zl, zr)
    zl_half, zr_half, both = arrange([zl, zr], [[(0, 0)], [(1, 1)], [(0, 0), (0, 1), (1, 0), (1, 1)]])
    both_xr, both_xl = move(both, 0, -1), move(both, 0, 1)
    z2b, z2a = move(zr_half, -1, 0), move(zl_half, 1, 0)
    shards = [shard(own), shard(xl), shard(xr), shard(x2), shard(both, 0), shard(both, 2)]
    first = score_call(next_kernel, shards, train_grads, blocks_shape(6, train_grads, queries))
    z2a, z2b, x2, first = in_order(z2a, z2b, x2, first)
    (z2,) = arrange([z2a, z2b], [[(0, 0), (1, 0)]], weight=20)
    z2_xl = move(z2, 0, 1)
    zr_x2, zl_x2 = move(x2, -1, 0), move(x2, 1, 0)
    z2, both_xr = in_order(z2, both_xr)
    z2_xr = move(z2, 0, -1)
    shards = [shard(z2), shard(both_xr, 0), shard(both_xr, 2)]
    second = score_call(next_kernel, shards, train_grads, blocks_shape(3, train_grads, queries))
    z2_xl, z2_xr, both_xl, zl_x2, zr_x2, second = in_order(z2_xl, z2_xr, both_xl, zl_x2, zr_x2, second)
    halves = arrange([z2_xl, z2_xr], [[(0, 0)], [(1, 1)]])
    z2_x2 = move(halves[0], 0, 1), move(halves[1], 0, -1)
    offsets = [
        (0, 0), (0, -1), (0, 1), (0, 2), (-1, 0), (1, 0),
        (2, 0), (-1, 1), (1, 1),
        (2, -1), (-1, -1), (1, -1),
        (2, 1), (-1, 2), (1, 2), (2, 2),
    ]
    shards = [shard(z2_xl), shard(both_xl, 0), shard(both_xl, 2)]
    shapes = [blocks_shape(3, train_grads, queries), jax.ShapeDtypeStruct(train_grads.shape, train_grads.dtype)]
    third, train = score_call(keep_kernel, shards, train_grads, shapes)
    third, train, *z2_x2 = in_order(third, train, *z2_x2)
    shards = [shard(z2_xr), shard(zl_x2), shard(zr_x2), [(half, 0) for half in z2_x2]]
    kernel = lambda own, count, *refs: last_kernel(own, count, offsets, *refs)
    shape = blocks_shape(SIDE * SIDE, train_grads, queries)
    parts = score_call(kernel, shards, train, shape, [first, second, third], [me])
    parts = lax.all_to_all(parts, "layer", split_axis=0, concat_axis=0, tiled=True)
    return jnp.sum(parts.astype(jnp.float32), axis=0)


def solution(mesh):
    in_specs = (
        P("layer", "ex", None),
        P("layer", "ex", None),
        P("layer", None, None),
        P("layer", None, None),
        P("layer", None, None),
    )
    out_specs = P("layer", "ex")
    return jax.shard_map(local, mesh=mesh, in_specs=in_specs, out_specs=out_specs, check_vma=False)
```

```python
import functools

import jax
import jax.numpy as jnp
from jax import lax
from jax.experimental import pallas as pl
from jax.experimental.pallas import tpu as pltpu
from jax.sharding import PartitionSpec as P

SIDE = 4
TILE = 2048

def split(v):
    hi = v.astype(jnp.bfloat16)
    return hi, (v - hi.astype(jnp.float32)).astype(jnp.bfloat16)

def twice(block):
    none = jnp.zeros_like(block)
    return jnp.concatenate([jnp.concatenate([block, none], axis=1), jnp.concatenate([none, block], axis=1)], axis=0)

def dot(a, b, dims=((1,), (0,))):
    return lax.dot_general(a, b, (dims, ((), ())), preferred_element_type=jnp.float32)

def precondition_kernel(raw, basis_out, basis_in, eigen, out, work):
    modules, count_q, entries = raw.shape
    side = basis_out.shape[1]
    half = count_q // 2
    low = lax.broadcasted_iota(jnp.int32, (half, 2 * side), 1) < side
    every = range(modules)
    nt = ((1,), (1,))

    outs = [split(basis_out[m]) for m in every]
    turned = [split(basis_out[m].T) for m in every]
    ins = [split(twice(basis_in[m])) for m in every]
    inverses = [1.0 / (eigen[m] + 0.1 * jnp.mean(eigen[m])) for m in every]
    inverses = [jnp.concatenate([v, v], axis=1) for v in inverses]
    for m in every:
        rows = []
        for pair in range(side // 2):
            tile = raw[m, :, pl.ds(pair * 2 * side, 2 * side)].astype(jnp.float32)
            top, bottom = tile[:half], tile[half:]
            rows.append(jnp.where(low, top, pltpu.roll(bottom, side, 1)))
            rows.append(jnp.where(low, pltpu.roll(top, side, 1), bottom))
        grads = jnp.concatenate(rows, axis=0).astype(jnp.bfloat16)
        work[m] = dot(jnp.concatenate([grads, grads], axis=1), jnp.concatenate(ins[m], axis=0))
    parts = []
    for m in every:
        left = jnp.concatenate([work[m, pl.ds(q, side, stride=half), :] for q in range(half)], axis=1)
        hi, lo = split(left)
        parts.append((hi, lo))
    rotated = []
    for m in every:
        (hi, lo), (t_hi, t_lo) = parts[m], turned[m]
        rotated.append(dot(jnp.concatenate([t_hi, t_hi, t_lo], axis=1), jnp.concatenate([hi, lo, hi], axis=0)))
    scaled = []
    for m in every:
        blocks = [rotated[m][:, q * 2 * side : (q + 1) * 2 * side] * inverses[m] for q in range(half)]
        scaled.append(split(jnp.concatenate(blocks, axis=1)))
    back = []
    for m in every:
        (hi, lo), (o_hi, o_lo) = scaled[m], outs[m]
        back.append(dot(jnp.concatenate([o_hi, o_hi, o_lo], axis=1), jnp.concatenate([hi, lo, hi], axis=0)))
    for m in every:
        hi, lo = split(jnp.concatenate([back[m][:, q * 2 * side : (q + 1) * 2 * side] for q in range(half)], axis=0))
        in_hi, in_lo = ins[m]
        work[m] = dot(jnp.concatenate([hi, lo], axis=1), jnp.concatenate([in_hi, in_hi], axis=1), nt) + dot(hi, in_lo, nt)
    for m in every:
        for pair in range(side // 2):
            even, odd = work[m, pl.ds(2 * pair, half, stride=side), :], work[m, pl.ds(2 * pair + 1, half, stride=side), :]
            at = pl.ds(pair * 2 * side, 2 * side)
            out[m, :half, at] = jnp.where(low, even, pltpu.roll(odd, side, 1)).astype(out.dtype)
            out[m, half:, at] = jnp.where(low, pltpu.roll(even, side, 1), odd).astype(out.dtype)

def precondition(raw, basis_out, basis_in, eigen):
    modules, count_q, entries = raw.shape
    side = basis_out.shape[1]
    full = lambda *shape: pl.BlockSpec(shape, lambda i: (0, 0, 0))
    return pl.pallas_call(
        precondition_kernel,
        out_shape=jax.ShapeDtypeStruct(raw.shape, jnp.bfloat16),
        grid=(1,),
        in_specs=[full(*raw.shape)] + [full(modules, side, side)] * 3,
        out_specs=full(*raw.shape),
        scratch_shapes=[pltpu.VMEM((modules, side * count_q // 2, 2 * side), jnp.float32)],
        compiler_params=pltpu.CompilerParams(vmem_limit_bytes=56 << 20),
    )(raw, basis_out, basis_in, eigen)


def move(value, step_z, step_x):
    to = lambda z, x: (z + step_z) % SIDE * SIDE + (x + step_x) % SIDE
    return lax.ppermute(value, "ex", [(z * SIDE + x, to(z, x)) for z in range(SIDE) for x in range(SIDE)])


def in_order(*values):
    return lax.optimization_barrier(values)


def cost(weight):
    return pl.CostEstimate(flops=int(weight * 1.1e9), bytes_accessed=1024, transcendentals=0)


def arrange(values, plan, weight=0):
    def kernel(*refs):
        given, made = refs[: len(values)], refs[len(values) :]
        for out, parts in zip(made, plan):
            for at, (value, module) in enumerate(parts):
                out[at] = given[value][module]

    space = pl.BlockSpec(memory_space=pltpu.VMEM)
    return pl.pallas_call(
        kernel,
        out_shape=[jax.ShapeDtypeStruct((len(parts),) + values[0].shape[1:], values[0].dtype) for parts in plan],
        in_specs=[space] * len(values),
        out_specs=[space] * len(plan),
        compiler_params=pltpu.CompilerParams(vmem_limit_bytes=4 << 20),
        cost_estimate=cost(weight),
    )(*values)


def blocks_of(shards, held, train, dtype, kept=None):
    total = None
    for module in range(train.shape[0]):
        for at in range(0, train.shape[2], TILE):
            part = pl.ds(at, TILE)
            stored = train[module, :, part]
            if kept is not None:
                kept[module, :, part] = stored
            rows = jnp.concatenate([held[s[module][0]][s[module][1], :, part] for s in shards], axis=0)
            term = dot(stored, rows, ((1,), (1,)))
            total = term if total is None else total + term
    return total.T.astype(dtype).reshape(len(shards), -1, train.shape[1])


def next_kernel(shards, count, *refs):
    held, (train, out) = refs[:count], refs[count:]
    out[...] = blocks_of(shards, held, train, out.dtype)


def last_kernel(shards, count, offsets, me, *refs):
    held, train, done, (keep, give) = refs[:count], refs[count], refs[count + 1 : -2], refs[-2:]
    z, x = lax.shift_right_logical(me[0], 2), me[0] & (SIDE - 1)
    places = [((z + dz) & (SIDE - 1)) * (SIDE // 2) + lax.shift_right_logical((x + dx) & (SIDE - 1), 1) for dz, dx in offsets]
    blocks = [(ref, i) for ref in done for i in range(ref.shape[0])]
    total = blocks_of(shards, held, train, keep.dtype)
    blocks += [(total, i) for i in range(len(shards))]
    for core in range(2):

        @pl.when(((x ^ me[1]) & 1) == core)
        def _():
            for (block, i), place, (_, dx) in zip(blocks, places, offsets):
                (keep if dx % 2 == core else give)[place] = block[i]


def score_call(kernel, shards, train, out_shapes, others=(), lead=(), weight=1):
    arrays = []
    for array in (array for shard in shards for array, _ in shard):
        if all(array is not a for a in arrays):
            arrays.append(array)
    number = lambda array: next(i for i, a in enumerate(arrays) if a is array)
    shards = [[(number(array), at) for array, at in shard] for shard in shards]
    space = pl.BlockSpec(memory_space=pltpu.VMEM)
    return pl.pallas_call(
        functools.partial(kernel, shards, len(arrays)),
        out_shape=out_shapes,
        in_specs=[pl.BlockSpec(memory_space=pltpu.SMEM)] * len(lead) + [space] * (len(arrays) + 1 + len(others)),
        out_specs=jax.tree.map(lambda _: space, out_shapes),
        compiler_params=pltpu.CompilerParams(vmem_limit_bytes=16 << 20),
        cost_estimate=cost(weight),
    )(*lead, *arrays, train, *others)


def shard(array, at=0):
    return [(array, at), (array, at + 1)]


def blocks_shape(count, train, queries):
    return jax.ShapeDtypeStruct((count, queries, train.shape[1]), jnp.float32)


def local(query_grads, train_grads, basis_out, basis_in, eigen):
    me = jnp.stack([lax.axis_index("ex"), lax.axis_index("layer")]).astype(jnp.int32)
    queries = query_grads.shape[1]
    own = precondition(query_grads, basis_out, basis_in, eigen)
    x2 = move(own, 0, 2)
    xr, xl = move(own, 0, -1), move(own, 0, 1)
    zr, zl = move(own, -1, 0), move(own, 1, 0)
    zl, zr = in_order(zl, zr)
    zl_half, zr_half, both = arrange([zl, zr], [[(0, 0)], [(1, 1)], [(0, 0), (0, 1), (1, 0), (1, 1)]])
    both_xr, both_xl = move(both, 0, -1), move(both, 0, 1)
    z2b, z2a = move(zr_half, -1, 0), move(zl_half, 1, 0)
    shards = [shard(own), shard(xl), shard(xr), shard(x2), shard(both, 0), shard(both, 2)]
    first = score_call(next_kernel, shards, train_grads, blocks_shape(6, train_grads, queries))
    z2a, z2b, x2, first = in_order(z2a, z2b, x2, first)
    (z2,) = arrange([z2a, z2b], [[(0, 0), (1, 0)]], weight=20)
    z2_xl = move(z2, 0, 1)
    zr_x2, zl_x2 = move(x2, -1, 0), move(x2, 1, 0)
    z2, both_xr = in_order(z2, both_xr)
    z2_xr = move(z2, 0, -1)
    shards = [shard(z2), shard(both_xr, 0), shard(both_xr, 2)]
    second = score_call(next_kernel, shards, train_grads, blocks_shape(3, train_grads, queries))
    z2_xl, z2_xr, both_xl, zl_x2, zr_x2, second = in_order(z2_xl, z2_xr, both_xl, zl_x2, zr_x2, second)
    halves = arrange([z2_xl, z2_xr], [[(0, 0)], [(1, 1)]])
    z2_x2 = move(halves[0], 0, 1), move(halves[1], 0, -1)
    offsets = [
        (0, 0), (0, -1), (0, 1), (0, 2), (-1, 0), (1, 0),
        (2, 0), (-1, 1), (1, 1),
        (2, -1), (-1, -1), (1, -1),
        (2, 1), (-1, 2), (1, 2), (2, 2),
    ]
    shards = [shard(z2_xl), shard(both_xl, 0), shard(both_xl, 2)]
    third = score_call(next_kernel, shards, train_grads, blocks_shape(3, train_grads, queries))
    third, *z2_x2 = in_order(third, *z2_x2)
    shards = [shard(z2_xr), shard(zl_x2), shard(zr_x2), [(half, 0) for half in z2_x2]]
    kernel = lambda own, count, *refs: last_kernel(own, count, offsets, *refs)
    shapes = [blocks_shape(SIDE * SIDE // 2, train_grads, queries)] * 2
    keep, give = score_call(kernel, shards, train_grads, shapes, [first, second, third], [me])
    count = lax.axis_size("layer")
    parts = keep + lax.ppermute(give, "layer", [(i, i ^ 1) for i in range(count)])
    groups = [list(range(core, count, 2)) for core in range(2)]
    parts = lax.all_to_all(
        parts.astype(jnp.bfloat16), "layer", split_axis=0, concat_axis=0, tiled=True, axis_index_groups=groups
    )
    return jnp.sum(parts.astype(jnp.float32), axis=0)


def solution(mesh):
    in_specs = (
        P("layer", "ex", None),
        P("layer", "ex", None),
        P("layer", None, None),
        P("layer", None, None),
        P("layer", None, None),
    )
    out_specs = P("layer", "ex")
    return jax.shard_map(local, mesh=mesh, in_specs=in_specs, out_specs=out_specs, check_vma=False)
```

```python
import functools

import jax
import jax.numpy as jnp
from jax import lax
from jax.experimental import pallas as pl
from jax.experimental.pallas import tpu as pltpu
from jax.sharding import PartitionSpec as P

SIDE = 4
TILE = 2048

def split(v):
    hi = v.astype(jnp.bfloat16)
    return hi, (v - hi.astype(jnp.float32)).astype(jnp.bfloat16)

def twice(block):
    none = jnp.zeros_like(block)
    return jnp.concatenate([jnp.concatenate([block, none], axis=1), jnp.concatenate([none, block], axis=1)], axis=0)

def dot(a, b, dims=((1,), (0,))):
    return lax.dot_general(a, b, (dims, ((), ())), preferred_element_type=jnp.float32)

def precondition_kernel(raw, basis_out, basis_in, eigen, out, work):
    modules, count_q, entries = raw.shape
    side = basis_out.shape[1]
    half = count_q // 2
    low = lax.broadcasted_iota(jnp.int32, (half, 2 * side), 1) < side
    every = range(modules)
    nt = ((1,), (1,))

    outs = [split(basis_out[m]) for m in every]
    turned = [split(basis_out[m].T) for m in every]
    ins = [split(twice(basis_in[m])) for m in every]
    inverses = [1.0 / (eigen[m] + 0.1 * jnp.mean(eigen[m])) for m in every]
    inverses = [jnp.concatenate([v, v], axis=1) for v in inverses]
    for m in every:
        rows = []
        for pair in range(side // 2):
            tile = raw[m, :, pl.ds(pair * 2 * side, 2 * side)].astype(jnp.float32)
            top, bottom = tile[:half], tile[half:]
            rows.append(jnp.where(low, top, pltpu.roll(bottom, side, 1)))
            rows.append(jnp.where(low, pltpu.roll(top, side, 1), bottom))
        grads = jnp.concatenate(rows, axis=0).astype(jnp.bfloat16)
        work[m] = dot(jnp.concatenate([grads, grads], axis=1), jnp.concatenate(ins[m], axis=0))
    parts = []
    for m in every:
        left = jnp.concatenate([work[m, pl.ds(q, side, stride=half), :] for q in range(half)], axis=1)
        hi, lo = split(left)
        parts.append((hi, lo))
    rotated = []
    for m in every:
        (hi, lo), (t_hi, t_lo) = parts[m], turned[m]
        rotated.append(dot(jnp.concatenate([t_hi, t_hi, t_lo], axis=1), jnp.concatenate([hi, lo, hi], axis=0)))
    scaled = []
    for m in every:
        blocks = [rotated[m][:, q * 2 * side : (q + 1) * 2 * side] * inverses[m] for q in range(half)]
        scaled.append(split(jnp.concatenate(blocks, axis=1)))
    back = []
    for m in every:
        (hi, lo), (o_hi, o_lo) = scaled[m], outs[m]
        back.append(dot(jnp.concatenate([o_hi, o_hi, o_lo], axis=1), jnp.concatenate([hi, lo, hi], axis=0)))
    for m in every:
        hi, lo = split(jnp.concatenate([back[m][:, q * 2 * side : (q + 1) * 2 * side] for q in range(half)], axis=0))
        in_hi, in_lo = ins[m]
        work[m] = dot(jnp.concatenate([hi, lo], axis=1), jnp.concatenate([in_hi, in_hi], axis=1), nt) + dot(hi, in_lo, nt)
    for m in every:
        for pair in range(side // 2):
            even, odd = work[m, pl.ds(2 * pair, half, stride=side), :], work[m, pl.ds(2 * pair + 1, half, stride=side), :]
            at = pl.ds(pair * 2 * side, 2 * side)
            out[m, :half, at] = jnp.where(low, even, pltpu.roll(odd, side, 1)).astype(out.dtype)
            out[m, half:, at] = jnp.where(low, pltpu.roll(even, side, 1), odd).astype(out.dtype)

def precondition(raw, basis_out, basis_in, eigen):
    modules, count_q, entries = raw.shape
    side = basis_out.shape[1]
    full = lambda *shape: pl.BlockSpec(shape, lambda i: (0, 0, 0))
    return pl.pallas_call(
        precondition_kernel,
        out_shape=jax.ShapeDtypeStruct(raw.shape, jnp.bfloat16),
        grid=(1,),
        in_specs=[full(*raw.shape)] + [full(modules, side, side)] * 3,
        out_specs=full(*raw.shape),
        scratch_shapes=[pltpu.VMEM((modules, side * count_q // 2, 2 * side), jnp.float32)],
        compiler_params=pltpu.CompilerParams(vmem_limit_bytes=56 << 20),
    )(raw, basis_out, basis_in, eigen)


def move(value, step_z, step_x):
    to = lambda z, x: (z + step_z) % SIDE * SIDE + (x + step_x) % SIDE
    return lax.ppermute(value, "ex", [(z * SIDE + x, to(z, x)) for z in range(SIDE) for x in range(SIDE)])


def in_order(*values):
    return lax.optimization_barrier(values)


def cost(weight):
    return pl.CostEstimate(flops=int(weight * 1.1e9), bytes_accessed=1024, transcendentals=0)


def arrange(values, plan, weight=0):
    def kernel(*refs):
        given, made = refs[: len(values)], refs[len(values) :]
        for out, parts in zip(made, plan):
            for at, (value, module) in enumerate(parts):
                out[at] = given[value][module]

    space = pl.BlockSpec(memory_space=pltpu.VMEM)
    return pl.pallas_call(
        kernel,
        out_shape=[jax.ShapeDtypeStruct((len(parts),) + values[0].shape[1:], values[0].dtype) for parts in plan],
        in_specs=[space] * len(values),
        out_specs=[space] * len(plan),
        compiler_params=pltpu.CompilerParams(vmem_limit_bytes=4 << 20),
        cost_estimate=cost(weight),
    )(*values)


def blocks_of(shards, held, train, dtype, kept=None):
    total = None
    for module in range(train.shape[0]):
        for at in range(0, train.shape[2], TILE):
            part = pl.ds(at, TILE)
            stored = train[module, :, part]
            if kept is not None:
                kept[module, :, part] = stored
            rows = jnp.concatenate([held[s[module][0]][s[module][1], :, part] for s in shards], axis=0)
            term = dot(stored, rows, ((1,), (1,)))
            total = term if total is None else total + term
    return total.T.astype(dtype).reshape(len(shards), -1, train.shape[1])


def next_kernel(shards, count, *refs):
    held, (train, out) = refs[:count], refs[count:]
    out[...] = blocks_of(shards, held, train, out.dtype)


def last_kernel(shards, count, offsets, me, *refs):
    held, train, done, (keep, give) = refs[:count], refs[count], refs[count + 1 : -2], refs[-2:]
    z, x = lax.shift_right_logical(me[0], 2), me[0] & (SIDE - 1)
    places = [((z + dz) & (SIDE - 1)) * (SIDE // 2) + lax.shift_right_logical((x + dx) & (SIDE - 1), 1) for dz, dx in offsets]
    blocks = [(ref, i) for ref in done for i in range(ref.shape[0])]
    total = blocks_of(shards, held, train, keep.dtype)
    blocks += [(total, i) for i in range(len(shards))]
    for core in range(2):

        @pl.when(((x ^ me[1]) & 1) == core)
        def _():
            for (block, i), place, (_, dx) in zip(blocks, places, offsets):
                (keep if dx % 2 == core else give)[place] = block[i]


def score_call(kernel, shards, train, out_shapes, others=(), lead=(), weight=1):
    arrays = []
    for array in (array for shard in shards for array, _ in shard):
        if all(array is not a for a in arrays):
            arrays.append(array)
    number = lambda array: next(i for i, a in enumerate(arrays) if a is array)
    shards = [[(number(array), at) for array, at in shard] for shard in shards]
    space = pl.BlockSpec(memory_space=pltpu.VMEM)
    return pl.pallas_call(
        functools.partial(kernel, shards, len(arrays)),
        out_shape=out_shapes,
        in_specs=[pl.BlockSpec(memory_space=pltpu.SMEM)] * len(lead) + [space] * (len(arrays) + 1 + len(others)),
        out_specs=jax.tree.map(lambda _: space, out_shapes),
        compiler_params=pltpu.CompilerParams(vmem_limit_bytes=16 << 20),
        cost_estimate=cost(weight),
    )(*lead, *arrays, train, *others)


def shard(array, at=0):
    return [(array, at), (array, at + 1)]


def blocks_shape(count, train, queries):
    return jax.ShapeDtypeStruct((count, queries, train.shape[1]), jnp.float32)


def local(query_grads, train_grads, basis_out, basis_in, eigen):
    me = jnp.stack([lax.axis_index("ex"), lax.axis_index("layer")]).astype(jnp.int32)
    queries = query_grads.shape[1]
    own = precondition(query_grads, basis_out, basis_in, eigen)
    x2 = move(own, 0, 2)
    xr, xl = move(own, 0, -1), move(own, 0, 1)
    zr, zl = move(own, -1, 0), move(own, 1, 0)
    zl, zr, xl, xr = in_order(zl, zr, xl, xr)
    zl_half, zr_half, both = arrange([zl, zr], [[(0, 0)], [(1, 1)], [(0, 0), (0, 1), (1, 0), (1, 1)]])
    both_xr, both_xl = move(both, 0, -1), move(both, 0, 1)
    z2b, z2a = move(zr_half, -1, 0), move(zl_half, 1, 0)
    shards = [shard(own), shard(xl), shard(xr), shard(x2), shard(both, 0), shard(both, 2)]
    first = score_call(next_kernel, shards, train_grads, blocks_shape(6, train_grads, queries), weight=10)
    z2a, z2b, x2, first = in_order(z2a, z2b, x2, first)
    (z2,) = arrange([z2a, z2b], [[(0, 0), (1, 0)]])
    z2_xl = move(z2, 0, 1)
    zr_x2, zl_x2 = move(x2, -1, 0), move(x2, 1, 0)
    z2, both_xr = in_order(z2, both_xr)
    z2_xr = move(z2, 0, -1)
    shards = [shard(z2), shard(both_xr, 0), shard(both_xr, 2)]
    second = score_call(next_kernel, shards, train_grads, blocks_shape(3, train_grads, queries))
    z2_xl, z2_xr, both_xl, zl_x2, zr_x2, second = in_order(z2_xl, z2_xr, both_xl, zl_x2, zr_x2, second)
    halves = arrange([z2_xl, z2_xr], [[(0, 0)], [(1, 1)]])
    z2_x2 = move(halves[0], 0, 1), move(halves[1], 0, -1)
    offsets = [
        (0, 0), (0, -1), (0, 1), (0, 2), (-1, 0), (1, 0),
        (2, 0), (-1, 1), (1, 1),
        (2, -1), (-1, -1), (1, -1),
        (2, 1), (-1, 2), (1, 2), (2, 2),
    ]
    shards = [shard(z2_xl), shard(both_xl, 0), shard(both_xl, 2)]
    third = score_call(next_kernel, shards, train_grads, blocks_shape(3, train_grads, queries))

    shards = [shard(z2_xr), shard(zl_x2), shard(zr_x2), [(half, 0) for half in z2_x2]]
    kernel = lambda own, count, *refs: last_kernel(own, count, offsets, *refs)
    shapes = [blocks_shape(SIDE * SIDE // 2, train_grads, queries)] * 2
    keep, give = score_call(kernel, shards, train_grads, shapes, [first, second, third], [me])
    count = lax.axis_size("layer")
    parts = keep + lax.ppermute(give, "layer", [(i, i ^ 1) for i in range(count)])
    groups = [list(range(core, count, 2)) for core in range(2)]
    parts = lax.all_to_all(
        parts.astype(jnp.bfloat16), "layer", split_axis=0, concat_axis=0, tiled=True, axis_index_groups=groups
    )
    return jnp.sum(parts.astype(jnp.float32), axis=0)


def solution(mesh):
    in_specs = (
        P("layer", "ex", None),
        P("layer", "ex", None),
        P("layer", None, None),
        P("layer", None, None),
        P("layer", None, None),
    )
    out_specs = P("layer", "ex")
    return jax.shard_map(local, mesh=mesh, in_specs=in_specs, out_specs=out_specs, check_vma=False)
```

```python
import functools

import jax
import jax.numpy as jnp
from jax import lax
from jax.experimental import pallas as pl
from jax.experimental.pallas import tpu as pltpu
from jax.sharding import PartitionSpec as P

SIDE = 4
TILE = 2048

def split(v):
    hi = v.astype(jnp.bfloat16)
    return hi, (v - hi.astype(jnp.float32)).astype(jnp.bfloat16)

def twice(block):
    none = jnp.zeros_like(block)
    return jnp.concatenate([jnp.concatenate([block, none], axis=1), jnp.concatenate([none, block], axis=1)], axis=0)

def dot(a, b, dims=((1,), (0,))):
    return lax.dot_general(a, b, (dims, ((), ())), preferred_element_type=jnp.float32)

def precondition_kernel(raw, basis_out, basis_in, eigen, out, work):
    modules, count_q, entries = raw.shape
    side = basis_out.shape[1]
    half = count_q // 2
    low = lax.broadcasted_iota(jnp.int32, (half, 2 * side), 1) < side
    every = range(modules)
    nt = ((1,), (1,))

    outs = [split(basis_out[m]) for m in every]
    turned = [split(basis_out[m].T) for m in every]
    ins = [split(twice(basis_in[m])) for m in every]
    inverses = [1.0 / (eigen[m] + 0.1 * jnp.mean(eigen[m])) for m in every]
    inverses = [jnp.concatenate([v, v], axis=1) for v in inverses]
    for m in every:
        rows = []
        for pair in range(side // 2):
            tile = raw[m, :, pl.ds(pair * 2 * side, 2 * side)].astype(jnp.float32)
            top, bottom = tile[:half], tile[half:]
            rows.append(jnp.where(low, top, pltpu.roll(bottom, side, 1)))
            rows.append(jnp.where(low, pltpu.roll(top, side, 1), bottom))
        grads = jnp.concatenate(rows, axis=0).astype(jnp.bfloat16)
        work[m] = dot(jnp.concatenate([grads, grads], axis=1), jnp.concatenate(ins[m], axis=0))
    parts = []
    for m in every:
        left = jnp.concatenate([work[m, pl.ds(q, side, stride=half), :] for q in range(half)], axis=1)
        hi, lo = split(left)
        parts.append((hi, lo))
    rotated = []
    for m in every:
        (hi, lo), (t_hi, t_lo) = parts[m], turned[m]
        rotated.append(dot(jnp.concatenate([t_hi, t_hi, t_lo], axis=1), jnp.concatenate([hi, lo, hi], axis=0)))
    scaled = []
    for m in every:
        blocks = [rotated[m][:, q * 2 * side : (q + 1) * 2 * side] * inverses[m] for q in range(half)]
        scaled.append(split(jnp.concatenate(blocks, axis=1)))
    back = []
    for m in every:
        (hi, lo), (o_hi, o_lo) = scaled[m], outs[m]
        back.append(dot(jnp.concatenate([o_hi, o_hi, o_lo], axis=1), jnp.concatenate([hi, lo, hi], axis=0)))
    for m in every:
        hi, lo = split(jnp.concatenate([back[m][:, q * 2 * side : (q + 1) * 2 * side] for q in range(half)], axis=0))
        in_hi, in_lo = ins[m]
        work[m] = dot(jnp.concatenate([hi, lo], axis=1), jnp.concatenate([in_hi, in_hi], axis=1), nt) + dot(hi, in_lo, nt)
    for m in every:
        for pair in range(side // 2):
            even, odd = work[m, pl.ds(2 * pair, half, stride=side), :], work[m, pl.ds(2 * pair + 1, half, stride=side), :]
            at = pl.ds(pair * 2 * side, 2 * side)
            out[m, :half, at] = jnp.where(low, even, pltpu.roll(odd, side, 1)).astype(out.dtype)
            out[m, half:, at] = jnp.where(low, pltpu.roll(even, side, 1), odd).astype(out.dtype)

def precondition(raw, basis_out, basis_in, eigen):
    modules, count_q, entries = raw.shape
    side = basis_out.shape[1]
    full = lambda *shape: pl.BlockSpec(shape, lambda i: (0, 0, 0))
    return pl.pallas_call(
        precondition_kernel,
        out_shape=jax.ShapeDtypeStruct(raw.shape, jnp.bfloat16),
        grid=(1,),
        in_specs=[full(*raw.shape)] + [full(modules, side, side)] * 3,
        out_specs=full(*raw.shape),
        scratch_shapes=[pltpu.VMEM((modules, side * count_q // 2, 2 * side), jnp.float32)],
        compiler_params=pltpu.CompilerParams(vmem_limit_bytes=56 << 20),
    )(raw, basis_out, basis_in, eigen)


def move(value, step_z, step_x):
    to = lambda z, x: (z + step_z) % SIDE * SIDE + (x + step_x) % SIDE
    return lax.ppermute(value, "ex", [(z * SIDE + x, to(z, x)) for z in range(SIDE) for x in range(SIDE)])


def in_order(*values):
    return lax.optimization_barrier(values)


def cost(weight):
    return pl.CostEstimate(flops=int(weight * 1.1e9), bytes_accessed=1024, transcendentals=0)


def arrange(values, plan, weight=0):
    def kernel(*refs):
        given, made = refs[: len(values)], refs[len(values) :]
        for out, parts in zip(made, plan):
            for at, (value, module) in enumerate(parts):
                out[at] = given[value][module]

    space = pl.BlockSpec(memory_space=pltpu.VMEM)
    return pl.pallas_call(
        kernel,
        out_shape=[jax.ShapeDtypeStruct((len(parts),) + values[0].shape[1:], values[0].dtype) for parts in plan],
        in_specs=[space] * len(values),
        out_specs=[space] * len(plan),
        compiler_params=pltpu.CompilerParams(vmem_limit_bytes=4 << 20),
        cost_estimate=cost(weight),
    )(*values)


def blocks_of(shards, held, train, dtype, kept=None):
    total = None
    for module in range(train.shape[0]):
        for at in range(0, train.shape[2], TILE):
            part = pl.ds(at, TILE)
            stored = train[module, :, part]
            if kept is not None:
                kept[module, :, part] = stored
            rows = jnp.concatenate([held[s[module][0]][s[module][1], :, part] for s in shards], axis=0)
            term = dot(stored, rows, ((1,), (1,)))
            total = term if total is None else total + term
    return total.T.astype(dtype).reshape(len(shards), -1, train.shape[1])


def next_kernel(shards, count, *refs):
    held, (train, out) = refs[:count], refs[count:]
    out[...] = blocks_of(shards, held, train, out.dtype)


def last_kernel(shards, count, offsets, me, *refs):
    held, train, done, (keep, give) = refs[:count], refs[count], refs[count + 1 : -2], refs[-2:]
    z, x = lax.shift_right_logical(me[0], 2), me[0] & (SIDE - 1)
    places = [((z + dz) & (SIDE - 1)) * (SIDE // 2) + lax.shift_right_logical((x + dx) & (SIDE - 1), 1) for dz, dx in offsets]
    blocks = [(ref, i) for ref in done for i in range(ref.shape[0])]
    total = blocks_of(shards, held, train, keep.dtype)
    blocks += [(total, i) for i in range(len(shards))]
    for core in range(2):

        @pl.when(((x ^ me[1]) & 1) == core)
        def _():
            for (block, i), place, (_, dx) in zip(blocks, places, offsets):
                (keep if dx % 2 == core else give)[place] = block[i]


def score_call(kernel, shards, train, out_shapes, others=(), lead=(), weight=1):
    arrays = []
    for array in (array for shard in shards for array, _ in shard):
        if all(array is not a for a in arrays):
            arrays.append(array)
    number = lambda array: next(i for i, a in enumerate(arrays) if a is array)
    shards = [[(number(array), at) for array, at in shard] for shard in shards]
    space = pl.BlockSpec(memory_space=pltpu.VMEM)
    return pl.pallas_call(
        functools.partial(kernel, shards, len(arrays)),
        out_shape=out_shapes,
        in_specs=[pl.BlockSpec(memory_space=pltpu.SMEM)] * len(lead) + [space] * (len(arrays) + 1 + len(others)),
        out_specs=jax.tree.map(lambda _: space, out_shapes),
        compiler_params=pltpu.CompilerParams(vmem_limit_bytes=16 << 20),
        cost_estimate=cost(weight),
    )(*lead, *arrays, train, *others)


def shard(array, at=0):
    return [(array, at), (array, at + 1)]


def blocks_shape(count, train, queries):
    return jax.ShapeDtypeStruct((count, queries, train.shape[1]), jnp.float32)


def local(query_grads, train_grads, basis_out, basis_in, eigen):
    me = jnp.stack([lax.axis_index("ex"), lax.axis_index("layer")]).astype(jnp.int32)
    queries = query_grads.shape[1]
    own = precondition(query_grads, basis_out, basis_in, eigen)
    x2 = move(own, 0, 2)
    xr, xl = move(own, 0, -1), move(own, 0, 1)
    zr, zl = move(own, -1, 0), move(own, 1, 0)
    zl, zr, xl, xr = in_order(zl, zr, xl, xr)
    zl_half, zr_half, both = arrange([zl, zr], [[(0, 0)], [(1, 1)], [(0, 0), (0, 1), (1, 0), (1, 1)]])
    both_xr, both_xl = move(both, 0, -1), move(both, 0, 1)
    z2b, z2a = move(zr_half, -1, 0), move(zl_half, 1, 0)
    shards = [shard(own), shard(xl), shard(xr), shard(x2), shard(both, 0), shard(both, 2)]
    first = score_call(next_kernel, shards, train_grads, blocks_shape(6, train_grads, queries), weight=10)
    z2a, z2b, x2, first = in_order(z2a, z2b, x2, first)
    (z2,) = arrange([z2a, z2b], [[(0, 0), (1, 0)]], weight=0)
    z2_xl = move(z2, 0, 1)
    zr_x2, zl_x2 = move(x2, -1, 0), move(x2, 1, 0)
    z2, both_xr = in_order(z2, both_xr)
    z2_xr = move(z2, 0, -1)
    shards = [shard(z2), shard(both_xr, 0), shard(both_xr, 2)]
    second = score_call(next_kernel, shards, train_grads, blocks_shape(3, train_grads, queries), weight=4)
    z2_xl, z2_xr, both_xl, zl_x2, zr_x2, second = in_order(z2_xl, z2_xr, both_xl, zl_x2, zr_x2, second)
    halves = arrange([z2_xl, z2_xr], [[(0, 0)], [(1, 1)]], weight=0)
    z2_x2 = move(halves[0], 0, 1), move(halves[1], 0, -1)
    offsets = [
        (0, 0), (0, -1), (0, 1), (0, 2), (-1, 0), (1, 0),
        (2, 0), (-1, 1), (1, 1),
        (2, -1), (-1, -1), (1, -1),
        (2, 1), (-1, 2), (1, 2), (2, 2),
    ]
    shards = [shard(z2_xl), shard(both_xl, 0), shard(both_xl, 2)]
    third = score_call(next_kernel, shards, train_grads, blocks_shape(3, train_grads, queries), weight=8)

    shards = [shard(z2_xr), shard(zl_x2), shard(zr_x2), [(half, 0) for half in z2_x2]]
    kernel = lambda own, count, *refs: last_kernel(own, count, offsets, *refs)
    shapes = [blocks_shape(SIDE * SIDE // 2, train_grads, queries)] * 2
    keep, give = score_call(kernel, shards, train_grads, shapes, [first, second, third], [me])
    count = lax.axis_size("layer")
    parts = keep + lax.ppermute(give, "layer", [(i, i ^ 1) for i in range(count)])
    groups = [list(range(core, count, 2)) for core in range(2)]
    parts = lax.all_to_all(
        parts.astype(jnp.bfloat16), "layer", split_axis=0, concat_axis=0, tiled=True, axis_index_groups=groups
    )
    return jnp.sum(parts.astype(jnp.float32), axis=0)


def solution(mesh):
    in_specs = (
        P("layer", "ex", None),
        P("layer", "ex", None),
        P("layer", None, None),
        P("layer", None, None),
        P("layer", None, None),
    )
    out_specs = P("layer", "ex")
    return jax.shard_map(local, mesh=mesh, in_specs=in_specs, out_specs=out_specs, check_vma=False)
```

```python
import functools

import jax
import jax.numpy as jnp
from jax import lax
from jax.experimental import pallas as pl
from jax.experimental.pallas import tpu as pltpu
from jax.sharding import PartitionSpec as P

SIDE = 4
TILE = 2048

def split(v):
    hi = v.astype(jnp.bfloat16)
    return hi, (v - hi.astype(jnp.float32)).astype(jnp.bfloat16)

def twice(block):
    none = jnp.zeros_like(block)
    return jnp.concatenate([jnp.concatenate([block, none], axis=1), jnp.concatenate([none, block], axis=1)], axis=0)

def dot(a, b, dims=((1,), (0,))):
    return lax.dot_general(a, b, (dims, ((), ())), preferred_element_type=jnp.float32)

def precondition_kernel(raw, basis_out, basis_in, eigen, out, work):
    modules, count_q, entries = raw.shape
    side = basis_out.shape[1]
    half = count_q // 2
    low = lax.broadcasted_iota(jnp.int32, (half, 2 * side), 1) < side
    every = range(modules)
    nt = ((1,), (1,))

    outs = [split(basis_out[m]) for m in every]
    turned = [split(basis_out[m].T) for m in every]
    ins = [split(twice(basis_in[m])) for m in every]
    inverses = [1.0 / (eigen[m] + 0.1 * jnp.mean(eigen[m])) for m in every]
    inverses = [jnp.concatenate([v, v], axis=1) for v in inverses]
    for m in every:
        rows = []
        for pair in range(side // 2):
            tile = raw[m, :, pl.ds(pair * 2 * side, 2 * side)].astype(jnp.float32)
            top, bottom = tile[:half], tile[half:]
            rows.append(jnp.where(low, top, pltpu.roll(bottom, side, 1)))
            rows.append(jnp.where(low, pltpu.roll(top, side, 1), bottom))
        grads = jnp.concatenate(rows, axis=0).astype(jnp.bfloat16)
        work[m] = dot(jnp.concatenate([grads, grads], axis=1), jnp.concatenate(ins[m], axis=0))
    parts = []
    for m in every:
        left = jnp.concatenate([work[m, pl.ds(q, side, stride=half), :] for q in range(half)], axis=1)
        hi, lo = split(left)
        parts.append((hi, lo))
    rotated = []
    for m in every:
        (hi, lo), (t_hi, t_lo) = parts[m], turned[m]
        rotated.append(dot(jnp.concatenate([t_hi, t_hi, t_lo], axis=1), jnp.concatenate([hi, lo, hi], axis=0)))
    scaled = []
    for m in every:
        blocks = [rotated[m][:, q * 2 * side : (q + 1) * 2 * side] * inverses[m] for q in range(half)]
        scaled.append(split(jnp.concatenate(blocks, axis=1)))
    back = []
    for m in every:
        (hi, lo), (o_hi, o_lo) = scaled[m], outs[m]
        back.append(dot(jnp.concatenate([o_hi, o_hi, o_lo], axis=1), jnp.concatenate([hi, lo, hi], axis=0)))
    for m in every:
        hi, lo = split(jnp.concatenate([back[m][:, q * 2 * side : (q + 1) * 2 * side] for q in range(half)], axis=0))
        in_hi, in_lo = ins[m]
        work[m] = dot(jnp.concatenate([hi, lo], axis=1), jnp.concatenate([in_hi, in_hi], axis=1), nt) + dot(hi, in_lo, nt)
    for m in every:
        for pair in range(side // 2):
            even, odd = work[m, pl.ds(2 * pair, half, stride=side), :], work[m, pl.ds(2 * pair + 1, half, stride=side), :]
            at = pl.ds(pair * 2 * side, 2 * side)
            out[m, :half, at] = jnp.where(low, even, pltpu.roll(odd, side, 1)).astype(out.dtype)
            out[m, half:, at] = jnp.where(low, pltpu.roll(even, side, 1), odd).astype(out.dtype)

def precondition(raw, basis_out, basis_in, eigen):
    modules, count_q, entries = raw.shape
    side = basis_out.shape[1]
    full = lambda *shape: pl.BlockSpec(shape, lambda i: (0, 0, 0))
    return pl.pallas_call(
        precondition_kernel,
        out_shape=jax.ShapeDtypeStruct(raw.shape, jnp.bfloat16),
        grid=(1,),
        in_specs=[full(*raw.shape)] + [full(modules, side, side)] * 3,
        out_specs=full(*raw.shape),
        scratch_shapes=[pltpu.VMEM((modules, side * count_q // 2, 2 * side), jnp.float32)],
        compiler_params=pltpu.CompilerParams(vmem_limit_bytes=56 << 20),
    )(raw, basis_out, basis_in, eigen)


def move(value, step_z, step_x):
    to = lambda z, x: (z + step_z) % SIDE * SIDE + (x + step_x) % SIDE
    return lax.ppermute(value, "ex", [(z * SIDE + x, to(z, x)) for z in range(SIDE) for x in range(SIDE)])


def in_order(*values):
    return lax.optimization_barrier(values)


def cost(weight):
    return pl.CostEstimate(flops=int(weight * 1.1e9), bytes_accessed=1024, transcendentals=0)


def arrange(values, plan, weight=0):
    def kernel(*refs):
        given, made = refs[: len(values)], refs[len(values) :]
        for out, parts in zip(made, plan):
            for at, (value, module) in enumerate(parts):
                out[at] = given[value][module]

    space = pl.BlockSpec(memory_space=pltpu.VMEM)
    return pl.pallas_call(
        kernel,
        out_shape=[jax.ShapeDtypeStruct((len(parts),) + values[0].shape[1:], values[0].dtype) for parts in plan],
        in_specs=[space] * len(values),
        out_specs=[space] * len(plan),
        compiler_params=pltpu.CompilerParams(vmem_limit_bytes=4 << 20),
        cost_estimate=cost(weight),
    )(*values)


def blocks_of(shards, held, train, dtype, kept=None):
    total = None
    for module in range(train.shape[0]):
        for at in range(0, train.shape[2], TILE):
            part = pl.ds(at, TILE)
            stored = train[module, :, part]
            if kept is not None:
                kept[module, :, part] = stored
            rows = jnp.concatenate([held[s[module][0]][s[module][1], :, part] for s in shards], axis=0)
            term = dot(stored, rows, ((1,), (1,)))
            total = term if total is None else total + term
    return total.T.astype(dtype).reshape(len(shards), -1, train.shape[1])


def next_kernel(shards, count, *refs):
    held, (train, out) = refs[:count], refs[count:]
    out[...] = blocks_of(shards, held, train, out.dtype)


def last_kernel(shards, count, offsets, me, *refs):
    held, train, done, (keep, give) = refs[:count], refs[count], refs[count + 1 : -2], refs[-2:]
    z, x = lax.shift_right_logical(me[0], 2), me[0] & (SIDE - 1)
    places = [((z + dz) & (SIDE - 1)) * (SIDE // 2) + lax.shift_right_logical((x + dx) & (SIDE - 1), 1) for dz, dx in offsets]
    blocks = [(ref, i) for ref in done for i in range(ref.shape[0])]
    total = blocks_of(shards, held, train, keep.dtype)
    blocks += [(total, i) for i in range(len(shards))]
    for core in range(2):

        @pl.when(((x ^ me[1]) & 1) == core)
        def _():
            for (block, i), place, (_, dx) in zip(blocks, places, offsets):
                (keep if dx % 2 == core else give)[place] = block[i]


def score_call(kernel, shards, train, out_shapes, others=(), lead=(), weight=1):
    arrays = []
    for array in (array for shard in shards for array, _ in shard):
        if all(array is not a for a in arrays):
            arrays.append(array)
    number = lambda array: next(i for i, a in enumerate(arrays) if a is array)
    shards = [[(number(array), at) for array, at in shard] for shard in shards]
    space = pl.BlockSpec(memory_space=pltpu.VMEM)
    return pl.pallas_call(
        functools.partial(kernel, shards, len(arrays)),
        out_shape=out_shapes,
        in_specs=[pl.BlockSpec(memory_space=pltpu.SMEM)] * len(lead) + [space] * (len(arrays) + 1 + len(others)),
        out_specs=jax.tree.map(lambda _: space, out_shapes),
        compiler_params=pltpu.CompilerParams(vmem_limit_bytes=16 << 20),
        cost_estimate=cost(weight),
    )(*lead, *arrays, train, *others)


def shard(array, at=0):
    return [(array, at), (array, at + 1)]


def blocks_shape(count, train, queries):
    return jax.ShapeDtypeStruct((count, queries, train.shape[1]), jnp.float32)


def local(query_grads, train_grads, basis_out, basis_in, eigen):
    me = jnp.stack([lax.axis_index("ex"), lax.axis_index("layer")]).astype(jnp.int32)
    queries = query_grads.shape[1]
    own = precondition(query_grads, basis_out, basis_in, eigen)
    x2 = move(own, 0, 2)
    xr, xl = move(own, 0, -1), move(own, 0, 1)
    zr, zl = move(own, -1, 0), move(own, 1, 0)
    zl, zr, xl, xr = in_order(zl, zr, xl, xr)
    zl_half, zr_half, both = arrange([zl, zr], [[(0, 0)], [(1, 1)], [(0, 0), (0, 1), (1, 0), (1, 1)]])
    both_xr, both_xl = move(both, 0, -1), move(both, 0, 1)
    z2b, z2a = move(zr_half, -1, 0), move(zl_half, 1, 0)
    shards = [shard(own), shard(xl), shard(xr), shard(x2), shard(both, 0), shard(both, 2)]
    first = score_call(next_kernel, shards, train_grads, blocks_shape(6, train_grads, queries), weight=10)
    z2a, z2b, x2, first = in_order(z2a, z2b, x2, first)
    (z2,) = arrange([z2a, z2b], [[(0, 0), (1, 0)]])
    z2_xl = move(z2, 0, 1)
    zr_x2, zl_x2 = move(x2, -1, 0), move(x2, 1, 0)
    z2, both_xr = in_order(z2, both_xr)
    z2_xr = move(z2, 0, -1)
    shards = [shard(z2), shard(both_xr, 0), shard(both_xr, 2)]
    second = score_call(next_kernel, shards, train_grads, blocks_shape(3, train_grads, queries), weight=6)
    z2_xl, z2_xr, both_xl, zl_x2, zr_x2, second = in_order(z2_xl, z2_xr, both_xl, zl_x2, zr_x2, second)
    halves = arrange([z2_xl, z2_xr], [[(0, 0)], [(1, 1)]])
    z2_x2 = move(halves[0], 0, 1), move(halves[1], 0, -1)
    offsets = [
        (0, 0), (0, -1), (0, 1), (0, 2), (-1, 0), (1, 0),
        (2, 0), (-1, 1), (1, 1),
        (2, -1), (-1, -1), (1, -1),
        (2, 1), (-1, 2), (1, 2), (2, 2),
    ]
    shards = [shard(z2_xl), shard(both_xl, 0), shard(both_xl, 2)]
    third = score_call(next_kernel, shards, train_grads, blocks_shape(3, train_grads, queries), weight=6)

    shards = [shard(z2_xr), shard(zl_x2), shard(zr_x2), [(half, 0) for half in z2_x2]]
    kernel = lambda own, count, *refs: last_kernel(own, count, offsets, *refs)
    shapes = [blocks_shape(SIDE * SIDE // 2, train_grads, queries)] * 2
    keep, give = score_call(kernel, shards, train_grads, shapes, [first, second, third], [me])
    count = lax.axis_size("layer")
    parts = keep + lax.ppermute(give, "layer", [(i, i ^ 1) for i in range(count)])
    groups = [list(range(core, count, 2)) for core in range(2)]
    parts = lax.all_to_all(
        parts.astype(jnp.bfloat16), "layer", split_axis=0, concat_axis=0, tiled=True, axis_index_groups=groups
    )
    return jnp.sum(parts.astype(jnp.float32), axis=0)


def solution(mesh):
    in_specs = (
        P("layer", "ex", None),
        P("layer", "ex", None),
        P("layer", None, None),
        P("layer", None, None),
        P("layer", None, None),
    )
    out_specs = P("layer", "ex")
    return jax.shard_map(local, mesh=mesh, in_specs=in_specs, out_specs=out_specs, check_vma=False)
```
